256 devices in a mesh: rep: 2 (over y_lo), dp: 16 (over z, core), tensor: 8 (over x, y_hi).
Axes of the slice: x: 4, y: 4 (y_hi: 2, y_lo: 2; y = y_hi * 2 + y_lo), z: 8, core: 2. Of those that a mesh axis runs over, the one named last changes fastest.
Arguments:
- z_act: bfloat16 [4096, 8192], P(('rep', 'dp'), 'tensor'), may hold values from -6 to 6
- x_act: bfloat16 [4096, 8192], P(('rep', 'dp'), 'tensor'), may hold values from -6 to 6
- b_act: bfloat16 [4096, 1024], P(('rep', 'dp'), 'tensor'), may hold values from -6 to 6
- c_act: bfloat16 [4096, 1024], P(('rep', 'dp'), 'tensor'), may hold values from -6 to 6
- dt_act: bfloat16 [4096, 128], P(('rep', 'dp'), 'tensor'), may hold values from -6 to 6
- segment: int32 [4096], P(('rep', 'dp')), may hold values from 0 to 15, as said below
- counts: int32 [32], P(('rep', 'dp')), may hold values from 32 to 128, as said below
- conv_x: float32 [4, 8192], P(None, 'tensor'), may hold values from -3 to 3
- conv_b: float32 [4, 1024], P(None, 'tensor'), may hold values from -3 to 3
- conv_c: float32 [4, 1024], P(None, 'tensor'), may hold values from -3 to 3
- a_log: float32 [128], P('tensor'), may hold values from -3 to 1.5
- dt_bias: float32 [128], P('tensor'), may hold values from -6 to -2
- d_skip: float32 [128], P('tensor'), may hold values from 0.5 to 1.5
- norm_gain: float32 [8192], P('tensor'), may hold values from 0.5 to 1.5
- w_out: bfloat16 [4096, 8192], P('dp', 'tensor'), may hold values from -0.0625 to 0.0625
- d_out: bfloat16 [4096, 4096], P(('rep', 'dp', 'tensor')), may hold values from -24 to 24
Outputs:
- grad_z: bfloat16 [4096, 8192], P(('rep', 'dp'), 'tensor')
- grad_x: bfloat16 [4096, 8192], P(('rep', 'dp'), 'tensor')
- grad_b: bfloat16 [4096, 1024], P(('rep', 'dp'), 'tensor')
- grad_c: bfloat16 [4096, 1024], P(('rep', 'dp'), 'tensor')
- grad_dt: bfloat16 [4096, 128], P(('rep', 'dp'), 'tensor')
- grad_conv_x: float32 [4, 8192], P(None, 'tensor')
- grad_conv_b: float32 [4, 1024], P(None, 'tensor')
- grad_conv_c: float32 [4, 1024], P(None, 'tensor')
- grad_a_log: float32 [128], P('tensor')
- grad_dt_bias: float32 [128], P('tensor')
- grad_d_skip: float32 [128], P('tensor')
- grad_norm_gain: float32 [8192], P('tensor')
- grad_w_out: float32 [4096, 8192], P('dp', 'tensor')
The draws below stay inside these ranges and needn't reach their ends.
Inputs may be any that keep to these rules, and one draw needn't show every extreme that they name: counts[j] is the number of live slots of shard j; some shard has exactly 128. Within each shard segment starts at 0 and never falls along the slots.
All inputs are finite; a program needn't handle non-finite values.
Results may differ from the reference program's by a relative error of at most 0.0055.
Values may be sent and summed in bfloat16 or wider, within the bound.
No kernel may reach another device: no remote copies, remote signals or barrier semaphores. Data moves between devices by JAX's collectives and lax.ppermute only.
A program may use at most 128 MiB of HBM per device.

```python
import jax
import jax.numpy as jnp
from jax import lax

D = 4096
HEADS = 128
HDIM = 64
NST = 128
SPAN = 128
KCONV = 4
CAP = 128
SHARDS = 32
TOKENS = 4096
INNER = 8192
STATE_COLS = 1024


def draw_counts(key, part):
    key = jax.random.fold_in(key, 11)
    first_key, second_key = jax.random.split(key)
    drawn_counts = jax.random.randint(first_key, (SHARDS,), CAP // 4, CAP + 1)
    fullest = jax.random.randint(second_key, (), 0, SHARDS)
    return jnp.where(jnp.arange(SHARDS) == fullest, CAP, drawn_counts).astype(jnp.int32)


def draw_segment(key, part):
    key = jax.random.fold_in(key, 12)
    first_key, second_key = jax.random.split(key)
    starts = jax.random.randint(first_key, (SHARDS, CAP), 0, 96) == 0
    positions = jnp.arange(CAP)
    starts = jnp.where(positions[None, :] == 0, True, starts)
    packed_shard = jax.random.randint(second_key, (), 0, SHARDS)
    regular = positions % 8 == 0
    starts = jnp.where((jnp.arange(SHARDS) == packed_shard)[:, None], regular[None, :], starts)
    numbers = jnp.cumsum(starts.astype(jnp.int32), axis=1) - 1
    numbers = jnp.minimum(numbers, CAP // 8 - 1)
    return numbers.reshape(TOKENS).astype(jnp.int32)


def raised(result, own_key, source, target, shards_of, factor):
    owner, partner = [(jnp.arange(result.shape[position]) // (result.shape[position] // shards_of)).reshape([-1 if axis == position else 1 for axis in range(result.ndim)]) for position in (source, target)]
    chosen = jax.random.permutation(own_key, shards_of)[partner]
    strong = (owner == chosen) | (owner == (partner + shards_of // 2) % shards_of)
    return jnp.where(strong, factor * result, result)


def steps_of(key, shape, pieces, smallest, top_value):
    loudness, own = 1.0, jax.random.fold_in(key, 6)
    for dim, shards_of in pieces:
        draws = jnp.exp(jax.random.uniform(jax.random.fold_in(own, dim), (shards_of,), jnp.float32, smallest / len(pieces), top_value / len(pieces)))
        loudness = loudness * jnp.repeat(draws, shape[dim] // shards_of).reshape([-1 if axis == dim else 1 for axis in range(len(shape))])
    return loudness


def centred(key, extent, width, bound, pieces=(), kind=jnp.bfloat16):
    level = steps_of(key, extent, pieces, -0.22, 0.18) if pieces else 1.0
    result = jax.random.normal(key, extent, jnp.float32) * width * level
    return jnp.minimum(jnp.maximum(result, -bound), bound).astype(kind)


def noise_with(stream_key, shape, scale, bound, cuts, heavy, kind=jnp.bfloat16):
    values = scale * jax.random.normal(stream_key, shape, jnp.float32)
    if cuts:
        values = values * steps_of(stream_key, shape, cuts, -0.22, 0.18)
    return jnp.clip(raised(values, jax.random.fold_in(stream_key, 3), *heavy), -bound, bound).astype(kind)


def setup_inputs(seed: int = 0) -> dict:
    seeds = jax.random.split(jax.random.key(seed), 17)
    z_act = centred(seeds[0], (TOKENS, INNER), 1.0, 6.0, ((0, 32), (1, 8)))
    x_act = centred(seeds[1], (TOKENS, INNER), 1.0, 6.0, ((0, 32), (1, 8)))
    b_act = centred(seeds[2], (TOKENS, STATE_COLS), 1.0, 6.0, ((0, 32), (1, 8)))
    c_act = centred(seeds[3], (TOKENS, STATE_COLS), 1.0, 6.0, ((0, 32), (1, 8)))
    dt_act = centred(seeds[4], (TOKENS, HEADS), 1.0, 6.0, ((0, 32), (1, 8)))
    segment = draw_segment(jax.random.fold_in(seeds[16], 71), 0)
    counts = draw_counts(jax.random.fold_in(seeds[16], 71), 0)
    conv_x = centred(seeds[7], (KCONV, INNER), KCONV ** -0.5, 3.0, ((1, 8),), jnp.float32)
    conv_b = centred(seeds[8], (KCONV, STATE_COLS), KCONV ** -0.5, 3.0, ((1, 8),), jnp.float32)
    conv_c = centred(seeds[9], (KCONV, STATE_COLS), KCONV ** -0.5, 3.0, ((1, 8),), jnp.float32)
    a_log = jnp.clip(-3.0 + 4.5 * jax.random.uniform(seeds[10], (HEADS,), jnp.float32) ** steps_of(seeds[10], (HEADS,), ((0, 8),), -0.2, 0.2), -3.0, 1.5)
    dt_bias = jnp.clip(-6.0 + 4.0 * jax.random.uniform(seeds[11], (HEADS,), jnp.float32) ** steps_of(seeds[11], (HEADS,), ((0, 8),), -0.2, 0.2), -6.0, -2.0)
    d_skip = jnp.clip(0.5 + 1.0 * jax.random.uniform(seeds[12], (HEADS,), jnp.float32) ** steps_of(seeds[12], (HEADS,), ((0, 8),), -0.2, 0.2), 0.5, 1.5)
    norm_gain = jnp.clip(1.0 + 0.1 * jax.random.normal(seeds[13], (INNER,), jnp.float32), 0.5, 1.5)
    w_out = centred(seeds[14], (D, INNER), INNER ** -0.5, 0.0625, ((0, 16), (1, 8)))
    d_out = noise_with(seeds[15], (TOKENS, D), 1.0, 24.0, ((0, 256),), (0, 1, 256, 6.0))
    return dict(z_act=z_act, x_act=x_act, b_act=b_act, c_act=c_act, dt_act=dt_act, segment=segment, counts=counts, conv_x=conv_x, conv_b=conv_b, conv_c=conv_c, a_log=a_log, dt_bias=dt_bias, d_skip=d_skip, norm_gain=norm_gain, w_out=w_out, d_out=d_out)


def conv_doc(values, taps, segment):
    length = values.shape[0]
    summed = jnp.zeros_like(values)
    for offset in range(KCONV):
        tap_index = KCONV - 1 - offset
        if offset == 0:
            shifted = values
            same_doc = segment == segment
        else:
            shifted = jnp.pad(values, ((offset, 0), (0, 0)))[:length]
            prior_seg = jnp.pad(segment, (offset, 0), constant_values=-1)[:length]
            same_doc = prior_seg == segment
        summed = summed + taps[tap_index][None, :] * jnp.where(same_doc[:, None], shifted, jnp.zeros_like(shifted))
    return jax.nn.silu(summed)

def span_step(carry, inputs):
    ssm_state, prior_seg = carry
    x_blk, b_blk, c_blk, dt_blk, la_blk, seg_blk = inputs
    head_count = x_blk.shape[1]
    per_group = head_count // b_blk.shape[1]
    highest = lax.Precision.HIGHEST
    cumul = jnp.cumsum(la_blk, axis=0)
    positions = jnp.arange(seg_blk.shape[0])
    causal = (positions[:, None] >= positions[None, :]) & (seg_blk[:, None] == seg_blk[None, :])
    log_gap = cumul.T[:, :, None] - cumul.T[:, None, :]
    decay_mat = jnp.exp(jnp.where(causal[None], log_gap, -1e+30))
    scores = jnp.einsum('tgn,sgn->gts', c_blk, b_blk, precision=highest)
    scores = jnp.repeat(scores, per_group, axis=0)
    weights = scores * decay_mat * dt_blk.T[:, None, :]
    intra_out = jnp.einsum('hts,shp->thp', weights, x_blk, precision=highest)
    keep_rows = (seg_blk == prior_seg).astype(cumul.dtype)
    c_heads = jnp.repeat(c_blk, per_group, axis=1)
    b_heads = jnp.repeat(b_blk, per_group, axis=1)
    inter_out = jnp.einsum('thn,hpn->thp', c_heads, ssm_state, precision=highest)
    inter_out = inter_out * (jnp.exp(cumul) * keep_rows[:, None])[:, :, None]
    last_seg = seg_blk[-1]
    tail_weight = jnp.exp(cumul[-1][None, :] - cumul) * dt_blk * (seg_blk == last_seg).astype(cumul.dtype)[:, None]
    fresh_state = jnp.einsum('sh,shp,shn->hpn', tail_weight, x_blk, b_heads, precision=highest)
    keep_state = (last_seg == prior_seg).astype(cumul.dtype)
    carried = keep_state * jnp.exp(cumul[-1])[:, None, None] * ssm_state
    return ((carried + fresh_state, last_seg), intra_out + inter_out)

def mixer_forward(z_act, x_act, b_act, c_act, dt_act, conv_x, conv_b, conv_c, a_log, dt_bias, d_skip, norm_gain, segment):
    length = x_act.shape[0]
    head_count = dt_act.shape[1]
    groups = b_act.shape[1] // NST
    x_conv = conv_doc(x_act.astype(jnp.float32), conv_x, segment)
    b_conv = conv_doc(b_act.astype(jnp.float32), conv_b, segment)
    c_conv = conv_doc(c_act.astype(jnp.float32), conv_c, segment)
    dt_step = jax.nn.softplus(dt_act.astype(jnp.float32) + dt_bias[None, :])
    log_decay = dt_step * (-jnp.exp(a_log))[None, :]
    blocks = length // SPAN
    span_inputs = (x_conv.reshape(blocks, SPAN, head_count, HDIM), b_conv.reshape(blocks, SPAN, groups, NST), c_conv.reshape(blocks, SPAN, groups, NST), dt_step.reshape(blocks, SPAN, head_count), log_decay.reshape(blocks, SPAN, head_count), segment.reshape(blocks, SPAN))
    initial = (jnp.zeros((head_count, HDIM, NST), jnp.float32), jnp.array(-1, jnp.int32))
    final_state, outputs = lax.scan(span_step, initial, span_inputs)
    ssm_out = outputs.reshape(length, head_count, HDIM) + d_skip[None, :, None] * x_conv.reshape(length, head_count, HDIM)
    gated_out = ssm_out.reshape(length, head_count * HDIM) * jax.nn.silu(z_act.astype(jnp.float32))
    grouped = gated_out.reshape(length, groups, -1)
    inv_rms = lax.rsqrt(lax.optimization_barrier(jnp.mean(grouped * grouped, axis=-1, keepdims=True)) + 1e-05)
    return (grouped * inv_rms).reshape(length, head_count * HDIM) * norm_gain[None, :]

def reference(z_act, x_act, b_act, c_act, dt_act, segment, counts, conv_x, conv_b, conv_c, a_log, dt_bias, d_skip, norm_gain, w_out, d_out):
    params = (conv_x, conv_b, conv_c, a_log, dt_bias, d_skip, norm_gain)
    stacked = (z_act.reshape(SHARDS, CAP, -1), x_act.reshape(SHARDS, CAP, -1), b_act.reshape(SHARDS, CAP, -1), c_act.reshape(SHARDS, CAP, -1), dt_act.reshape(SHARDS, CAP, -1), segment.reshape(SHARDS, CAP), counts, d_out.reshape(SHARDS, CAP, D))

    def one_shard(totals, items):
        z_part, x_part, b_part, c_part, dt_part, seg_part, count_part, out_part = items
        live_rows = jnp.arange(CAP) < count_part
        masked = jnp.where(live_rows[:, None], out_part, jnp.zeros_like(out_part))

        def forward(activations, weights):
            return mixer_forward(activations[0], activations[1], activations[2], activations[3], activations[4], weights[0], weights[1], weights[2], weights[3], weights[4], weights[5], weights[6], seg_part)
        normed, pullback = jax.vjp(forward, (z_part, x_part, b_part, c_part, dt_part), params)
        normed_b = normed.astype(jnp.bfloat16)
        upstream = jnp.dot(masked, w_out, preferred_element_type=jnp.float32)
        act_grads, param_grads = pullback(upstream)
        weight_grad = jnp.dot(masked.T, normed_b, preferred_element_type=jnp.float32)
        new_totals = (jax.tree.map(lambda first_term, second_term: first_term + second_term, totals[0], param_grads), totals[1] + weight_grad)
        return (new_totals, act_grads)
    initial = (jax.tree.map(jnp.zeros_like, params), jnp.zeros((D, INNER), jnp.float32))
    totals, act_grads = lax.scan(one_shard, initial, stacked)
    grad_z = act_grads[0].reshape(TOKENS, -1)
    grad_x = act_grads[1].reshape(TOKENS, -1)
    grad_b = act_grads[2].reshape(TOKENS, -1)
    grad_c = act_grads[3].reshape(TOKENS, -1)
    grad_dt = act_grads[4].reshape(TOKENS, -1)
    sums = totals[0]
    return (grad_z, grad_x, grad_b, grad_c, grad_dt, sums[0], sums[1], sums[2], sums[3], sums[4], sums[5], sums[6], totals[1])
```

```python
import jax
import jax.numpy as jnp
from jax import lax
from jax.experimental import pallas as pl
from jax.experimental.pallas import tpu as pltpu
from jax.sharding import PartitionSpec as P

HDIM = 64
LANES = 128
KCONV = 4
EPS = 1e-05
F32 = jnp.float32
BF16 = jnp.bfloat16
VMEM_LIMIT = 48 * 1024 * 1024


def split2(value):
    high = value.astype(BF16)
    low = (value - high.astype(F32)).astype(BF16)
    return high, low


def split3(value):
    high = value.astype(BF16)
    rest = value - high.astype(F32)
    middle = rest.astype(BF16)
    low = (rest - middle.astype(F32)).astype(BF16)
    return high, middle, low


def dot_nn(left, right):
    left_h, left_l = split2(left)
    right_h, right_l = split2(right)
    return jnp.dot(
        jnp.concatenate([left_h, left_h, left_l], axis=1),
        jnp.concatenate([right_h, right_l, right_h], axis=0),
        preferred_element_type=F32,
    )


def dot_nt(left, right):
    left_h, left_l = split2(left)
    right_h, right_l = split2(right)
    return lax.dot_general(
        jnp.concatenate([left_h, left_h, left_l], axis=1),
        jnp.concatenate([right_h, right_l, right_h], axis=1),
        (((1,), (1,)), ((), ())),
        preferred_element_type=F32,
    )


def dot_exact(left_pieces, right):
    total = jnp.dot(left_pieces[0], right, preferred_element_type=F32)
    for piece in left_pieces[1:]:
        total = total + jnp.dot(piece, right, preferred_element_type=F32)
    return total


def sigmoid(value):
    return 1.0 / (1.0 + jnp.exp(-value))


def iota(axis, shape=(LANES, LANES)):
    return lax.broadcasted_iota(jnp.int32, shape, axis)


def shift_masks(seg_row):
    seg_cols = jnp.broadcast_to(seg_row.astype(F32), (LANES, LANES))
    seg_rows = seg_cols.T
    rows = iota(0)
    masks = []
    for offset in range(1, KCONV):
        prior = pltpu.roll(seg_rows, offset, 0)
        masks.append(jnp.where((rows >= offset) & (prior == seg_rows), 1.0, 0.0).astype(F32))
    return seg_rows, seg_cols, masks


def conv_silu(values, taps, masks):
    summed = taps[KCONV - 1 : KCONV] * values
    for offset in range(1, KCONV):
        shifted = pltpu.roll(values, offset, 0) * masks[offset - 1]
        summed = summed + taps[KCONV - 1 - offset : KCONV - offset] * shifted
    sig = sigmoid(summed)
    return summed * sig, sig * (1.0 + summed * (1.0 - sig))


def conv_back(cotangent, values, taps, masks):
    result = taps[KCONV - 1 : KCONV] * cotangent
    tap_grads = [None] * KCONV
    tap_grads[KCONV - 1] = jnp.sum(cotangent * values, axis=0, keepdims=True)
    for offset in range(1, KCONV):
        moved = pltpu.roll(cotangent * masks[offset - 1], LANES - offset, 0)
        result = result + taps[KCONV - 1 - offset : KCONV - offset] * moved
        tap_grads[KCONV - 1 - offset] = jnp.sum(moved * values, axis=0, keepdims=True)
    return result, tap_grads


def head_expander(heads):
    shape = (heads, heads * HDIM)
    return jnp.where(iota(1, shape) // HDIM == iota(0, shape), 1.0, 0.0).astype(BF16)


def two_halves(value):
    left = iota(1) < HDIM
    zero = jnp.zeros_like(value)
    return jnp.concatenate([jnp.where(left, value, zero), jnp.where(left, zero, value)], axis=0)


def forward_kernel(
    count_ref, z_ref, x_ref, b_ref, c_ref, dt_ref, seg_ref, cx_ref, cb_ref, cc_ref, al_ref, bias_ref, skip_ref, gain_ref,
    norm_ref, xc_ref, dsx_ref, ssm_ref, gate_ref, dgate_ref, bcc_ref, small_ref, cumt_ref, rms_ref,
):
    heads = dt_ref.shape[1]
    tiles = x_ref.shape[1] // LANES
    seg_rows, seg_cols, masks = shift_masks(seg_ref[...])
    rows, cols = iota(0), iota(1)
    causal = (rows >= cols) & (seg_rows == seg_cols)

    b_conv, b_slope = conv_silu(b_ref[...].astype(F32), cb_ref[...], masks)
    c_conv, c_slope = conv_silu(c_ref[...].astype(F32), cc_ref[...], masks)
    bcc_ref[0] = b_conv
    bcc_ref[1] = c_conv
    bcc_ref[2] = b_slope
    bcc_ref[3] = c_slope
    scores = dot_nt(c_conv, b_conv)
    bcc_ref[4] = scores.T

    raw = dt_ref[...].astype(F32) + bias_ref[...]
    step = jnp.maximum(raw, 0.0) + jnp.log1p(jnp.exp(-jnp.abs(raw)))
    decay = -jnp.exp(al_ref[...]) * step
    lower = jnp.where(rows >= cols, 1.0, 0.0).astype(BF16)
    cumul = sum(jnp.dot(lower, piece, preferred_element_type=F32) for piece in split3(decay))
    cumul_t = cumul.T
    cumt_ref[...] = cumul_t
    small_ref[0] = step
    small_ref[1] = decay
    small_ref[2] = cumul
    small_ref[3] = sigmoid(raw)

    expander = head_expander(heads)
    step_wide = dot_exact(split3(step), expander)
    skip_wide = dot_exact(split3(jnp.broadcast_to(skip_ref[...], (8, heads))), expander)

    squares = jnp.zeros((LANES, LANES), F32)
    for tile in range(tiles):
        span = slice(tile * LANES, (tile + 1) * LANES)
        x_conv, x_slope = conv_silu(x_ref[:, span].astype(F32), cx_ref[:, span], masks)
        xc_ref[:, span] = x_conv
        dsx_ref[:, span] = x_slope
        pieces = []
        for head in (2 * tile, 2 * tile + 1):
            gap = cumul[:, head : head + 1] - cumul_t[head : head + 1, :]
            pieces.append(scores * jnp.exp(jnp.where(causal, gap, -1e30)))
        weights = jnp.concatenate(pieces, axis=1)
        ssm = dot_nn(weights, two_halves(step_wide[:, span] * x_conv))
        ssm = ssm + skip_wide[0:1, span] * x_conv
        ssm_ref[:, span] = ssm
        z_tile = z_ref[:, span].astype(F32)
        sig = sigmoid(z_tile)
        gate = z_tile * sig
        gate_ref[:, span] = gate
        dgate_ref[:, span] = sig * (1.0 + z_tile * (1.0 - sig))
        gated = ssm * gate
        squares = squares + gated * gated
    mean = jnp.sum(squares, axis=1, keepdims=True) / (tiles * LANES)
    inv = lax.rsqrt(jnp.broadcast_to(mean, (LANES, LANES)) + EPS)
    rms_ref[...] = inv
    alive = jnp.where(rows < count_ref[0], 1.0, 0.0).astype(F32)
    for tile in range(tiles):
        span = slice(tile * LANES, (tile + 1) * LANES)
        normed = ssm_ref[:, span] * gate_ref[:, span] * inv * gain_ref[:, span]
        norm_ref[:, span] = (normed * alive).astype(BF16)


def backward_kernel(
    count_ref, up_ref, x_ref, b_ref, c_ref, seg_ref, cx_ref, cb_ref, cc_ref, al_ref, skip_ref, gain_ref,
    xc_ref, dsx_ref, ssm_ref, gate_ref, dgate_ref, bcc_ref, small_ref, cumt_ref, rms_ref,
    gz_ref, gx_ref, gb_ref, gc_ref, gdt_ref, par_ref,
):
    heads = small_ref.shape[2]
    tiles = x_ref.shape[1] // LANES
    seg_rows, seg_cols, masks = shift_masks(seg_ref[...])
    rows, cols = iota(0), iota(1)
    causal_t = (cols >= rows) & (seg_rows == seg_cols)
    alive = jnp.where(rows < count_ref[0], 1.0, 0.0).astype(F32)
    inv = rms_ref[...]
    scores_t = bcc_ref[4]
    step, decay, cumul, slope = small_ref[0], small_ref[1], small_ref[2], small_ref[3]
    cumul_t = cumt_ref[...]
    expander = head_expander(heads)
    step_wide = dot_exact(split3(step), expander)
    skip_wide = dot_exact(split3(jnp.broadcast_to(skip_ref[...], (8, heads))), expander)

    dots = jnp.zeros((LANES, LANES), F32)
    for tile in range(tiles):
        span = slice(tile * LANES, (tile + 1) * LANES)
        upstream = up_ref[:, span] * alive
        gated = ssm_ref[:, span] * gate_ref[:, span]
        product = upstream * gated
        dots = dots + product * gain_ref[:, span]
        par_ref[32 + tile : 33 + tile, :] = jnp.sum(product * inv, axis=0, keepdims=True)
    mean = jnp.sum(dots, axis=1, keepdims=True) / (tiles * LANES)
    pull = jnp.broadcast_to(mean, (LANES, LANES)) * inv * inv * inv

    before = jnp.where(rows > cols, 1.0, 0.0).astype(BF16)
    before = jnp.concatenate([before, before], axis=1)
    after = jnp.where(cols >= rows, 1.0, 0.0).astype(F32)
    score_grad = jnp.zeros((LANES, LANES), F32)
    sums = jnp.zeros((LANES, LANES), F32)
    for tile in range(tiles):
        span = slice(tile * LANES, (tile + 1) * LANES)
        x_conv = xc_ref[:, span]
        ssm = ssm_ref[:, span]
        gate = gate_ref[:, span]
        d_gated = inv * (up_ref[:, span] * alive) * gain_ref[:, span] - ssm * gate * pull
        gz_ref[:, span] = (d_gated * ssm * dgate_ref[:, span]).astype(BF16)
        d_ssm = d_gated * gate
        x_step = step_wide[:, span] * x_conv
        d_weights = dot_nt(two_halves(x_step), d_ssm)
        pieces = []
        for which in range(2):
            head = 2 * tile + which
            gap = cumul_t[head : head + 1, :] - cumul[:, head : head + 1]
            fade = jnp.exp(jnp.where(causal_t, gap, -1e30))
            d_weight = d_weights[which * LANES : (which + 1) * LANES, :] * fade
            score_grad = score_grad + d_weight
            pieces.append((scores_t * fade, d_weight * scores_t))
        d_xstep = dot_nn(
            jnp.concatenate([pieces[0][0], pieces[1][0]], axis=1), two_halves(d_ssm)
        )
        gaps_h, gaps_l = split2(jnp.concatenate([pieces[0][1], pieces[1][1]], axis=1))
        gaps = jnp.dot(
            before, jnp.concatenate([gaps_h, gaps_l], axis=0), preferred_element_type=F32
        )
        terms = (
            gaps[:, :LANES] * after,
            gaps[:, LANES:] * after,
            d_xstep * x_conv,
            d_ssm * x_conv,
        )
        pickers = (
            jnp.where(cols == 2 * tile, 1.0, 0.0),
            jnp.where(cols == 2 * tile + 1, 1.0, 0.0),
            jnp.where(cols == heads + 2 * tile + rows // HDIM, 1.0, 0.0),
            jnp.where(cols == 2 * heads + 2 * tile + rows // HDIM, 1.0, 0.0),
        )
        left, right = [], []
        for term, picker in zip(terms, pickers):
            term_h, term_l = split2(term)
            left += [term_h, term_l]
            right += [picker.astype(BF16)] * 2
        sums = sums + jnp.dot(
            jnp.concatenate(left, axis=1),
            jnp.concatenate(right, axis=0),
            preferred_element_type=F32,
        )
        d_conv = skip_wide[0:1, span] * d_ssm + step_wide[:, span] * d_xstep
        x_grad, tap_grads = conv_back(
            d_conv * dsx_ref[:, span], x_ref[:, span].astype(F32), cx_ref[:, span], masks
        )
        gx_ref[:, span] = x_grad.astype(BF16)
        for tap in range(KCONV):
            par_ref[tap * tiles + tile : tap * tiles + tile + 1, :] = tap_grads[tap]

    d_decay = sums[:, 0:heads]
    d_step = sums[:, heads : 2 * heads] - jnp.exp(al_ref[...]) * d_decay
    d_raw = d_step * slope
    gdt_ref[...] = d_raw.astype(BF16)
    par_ref[48:49, 0:heads] = jnp.sum(d_decay * decay, axis=0, keepdims=True)
    par_ref[49:50, 0:heads] = jnp.sum(d_raw, axis=0, keepdims=True)
    par_ref[50:51, 0:heads] = jnp.sum(sums[:, 2 * heads : 3 * heads], axis=0, keepdims=True)

    b_conv, c_conv = bcc_ref[0], bcc_ref[1]
    b_grad, tap_grads = conv_back(
        dot_nn(score_grad, c_conv) * bcc_ref[2], b_ref[...].astype(F32), cb_ref[...], masks
    )
    gb_ref[...] = b_grad.astype(BF16)
    for tap in range(KCONV):
        par_ref[40 + tap : 41 + tap, :] = tap_grads[tap]
    c_grad, tap_grads = conv_back(
        dot_nn(score_grad.T, b_conv) * bcc_ref[3], c_ref[...].astype(F32), cc_ref[...], masks
    )
    gc_ref[...] = c_grad.astype(BF16)
    for tap in range(KCONV):
        par_ref[44 + tap : 45 + tap, :] = tap_grads[tap]


def unpack_kernel(par_ref, cx_ref, cb_ref, cc_ref, al_ref, bias_ref, skip_ref, gain_ref):
    heads = al_ref.shape[1]
    tiles = cx_ref.shape[1] // LANES
    total = par_ref[...]
    for tap in range(KCONV):
        for tile in range(tiles):
            cx_ref[tap : tap + 1, tile * LANES : (tile + 1) * LANES] = total[
                tap * tiles + tile : tap * tiles + tile + 1
            ]
    for tile in range(tiles):
        gain_ref[:, tile * LANES : (tile + 1) * LANES] = total[32 + tile : 33 + tile]
    cb_ref[...] = total[40:44]
    cc_ref[...] = total[44:48]
    al_ref[...] = total[48:49, 0:heads]
    bias_ref[...] = total[49:50, 0:heads]
    skip_ref[...] = total[50:51, 0:heads]


def call(kernel, operands, outs, flops, smem_first=True):
    vmem = pl.BlockSpec(memory_space=pltpu.VMEM)
    specs = [vmem] * len(operands)
    if smem_first:
        specs[0] = pl.BlockSpec(memory_space=pltpu.SMEM)
    size = sum(a.size * a.dtype.itemsize for a in operands) + sum(
        a.size * a.dtype.itemsize for a in outs
    )
    return pl.pallas_call(
        kernel,
        out_shape=outs,
        in_specs=specs,
        out_specs=[vmem] * len(outs),
        compiler_params=pltpu.CompilerParams(vmem_limit_bytes=VMEM_LIMIT),
        cost_estimate=pl.CostEstimate(flops=flops, bytes_accessed=size, transcendentals=0),
    )(*operands)


def shape(dims, dtype=F32):
    return jax.ShapeDtypeStruct(dims, dtype)


def swap(value, axis, bit, size):
    return lax.ppermute(value, axis, [(i, i ^ bit) for i in range(size)])


def gather_tensor(block, axis):
    me = lax.axis_index("tensor")
    held = jnp.expand_dims(block, axis)
    for bit in (1, 2, 4):
        other = swap(held, "tensor", bit, 8)
        first = (me & bit) == 0
        held = jnp.concatenate(
            [jnp.where(first, held, other), jnp.where(first, other, held)], axis=axis
        )
    return held


def body(
    z_act, x_act, b_act, c_act, dt_act, segment, counts,
    conv_x, conv_b, conv_c, a_log, dt_bias, d_skip, norm_gain, w_out, d_out,
):
    length, width = z_act.shape
    heads = dt_act.shape[1]
    features = d_out.shape[1]
    dp = lax.axis_size("dp")
    seg_row = segment.reshape(1, length)
    a_log, dt_bias, d_skip = (v.reshape(1, heads) for v in (a_log, dt_bias, d_skip))
    gain = norm_gain.reshape(1, width)

    w_all = lax.all_gather(w_out, "dp", axis=0, tiled=True)

    own = d_out.shape[0]
    rows = gather_tensor(d_out, 0).reshape(length, features)
    pieces = d_out.reshape(own, dp, features // dp).transpose(1, 0, 2)
    pieces = lax.all_to_all(pieces, "dp", 0, 0, tiled=False)
    columns = gather_tensor(pieces, 1).reshape(dp * length, features // dp)

    wide = shape((length, width))
    normed, *saved = call(
        forward_kernel,
        (counts, z_act, x_act, b_act, c_act, dt_act, seg_row, conv_x, conv_b, conv_c, a_log, dt_bias, d_skip, gain),
        [
            shape((length, width), BF16), wide, wide, wide, wide, wide,
            shape((5, LANES, LANES)), shape((4, length, heads)), shape((heads, length)), shape((LANES, LANES)),
        ],
        300_000_000,
    )
    normed_all = lax.all_gather(normed, "dp", axis=0, tiled=True)

    upstream = jnp.dot(rows, w_all, preferred_element_type=F32)
    *act_grads, packed = call(
        backward_kernel,
        (counts, upstream, x_act, b_act, c_act, seg_row, conv_x, conv_b, conv_c, a_log, d_skip, gain, *saved),
        [
            shape((length, width), BF16), shape((length, width), BF16), shape((length, LANES), BF16),
            shape((length, LANES), BF16), shape((length, heads), BF16), shape((56, LANES)),
        ],
        600_000_000,
    )
    packed = packed + swap(packed, "dp", 1, dp)
    packed = packed + swap(packed, "rep", 1, 2)
    for bit in (2, 4, 8):
        packed = packed + swap(packed, "dp", bit, dp)
    sums = call(
        unpack_kernel,
        (packed,),
        [
            shape(conv_x.shape), shape(conv_b.shape), shape(conv_c.shape),
            shape((1, heads)), shape((1, heads)), shape((1, heads)), shape((1, width)),
        ],
        1000,
        smem_first=False,
    )

    share = lax.dot_general(
        columns, normed_all, (((0,), (0,)), ((), ())), preferred_element_type=F32
    ).astype(BF16)
    weight_grad = share.astype(F32) + swap(share, "rep", 1, 2).astype(F32)
    return (
        *act_grads,
        sums[0], sums[1], sums[2],
        sums[3].reshape(heads), sums[4].reshape(heads), sums[5].reshape(heads), sums[6].reshape(width),
        weight_grad,
    )


def solution(mesh):
    tokens = P(("rep", "dp"), "tensor")
    shards = P(("rep", "dp"))
    taps = P(None, "tensor")
    per_head = P("tensor")
    weight = P("dp", "tensor")
    in_specs = (
        *([tokens] * 5), shards, shards, *([taps] * 3), *([per_head] * 4),
        weight, P(("rep", "dp", "tensor"), None),
    )
    out_specs = (*([tokens] * 5), *([taps] * 3), *([per_head] * 4), weight)
    return jax.shard_map(body, mesh=mesh, in_specs=in_specs, out_specs=out_specs, check_vma=False)
```

```python
import jax
import jax.numpy as jnp
from jax import lax
from jax.experimental import pallas as pl
from jax.experimental.pallas import tpu as pltpu
from jax.sharding import PartitionSpec as P

HDIM = 64
LANES = 128
KCONV = 4
CHUNKS = 8
FORWARD_ARGS = 13
EPS = 1e-05
F32 = jnp.float32
BF16 = jnp.bfloat16
MIB = 1024 * 1024


def split2(value):
    high = value.astype(BF16)
    low = (value - high.astype(F32)).astype(BF16)
    return high, low


def split3(value):
    high = value.astype(BF16)
    rest = value - high.astype(F32)
    middle = rest.astype(BF16)
    low = (rest - middle.astype(F32)).astype(BF16)
    return high, middle, low


def dot_nn(left, right):
    left_h, left_l = split2(left)
    right_h, right_l = split2(right)
    return jnp.dot(
        jnp.concatenate([left_h, left_h, left_l], axis=1),
        jnp.concatenate([right_h, right_l, right_h], axis=0),
        preferred_element_type=F32,
    )


def dot_nt(left, right):
    left_h, left_l = split2(left)
    right_h, right_l = split2(right)
    return lax.dot_general(
        jnp.concatenate([left_h, left_h, left_l], axis=1),
        jnp.concatenate([right_h, right_l, right_h], axis=1),
        (((1,), (1,)), ((), ())),
        preferred_element_type=F32,
    )


def dot_exact(left_pieces, right):
    total = jnp.dot(left_pieces[0], right, preferred_element_type=F32)
    for piece in left_pieces[1:]:
        total = total + jnp.dot(piece, right, preferred_element_type=F32)
    return total


def sigmoid(value):
    return 1.0 / (1.0 + jnp.exp(-value))


def iota(axis, shape=(LANES, LANES)):
    return lax.broadcasted_iota(jnp.int32, shape, axis)


def shift_masks(seg_row):
    seg_cols = jnp.broadcast_to(seg_row.astype(F32), (LANES, LANES))
    seg_rows = seg_cols.T
    rows = iota(0)
    masks = []
    for offset in range(1, KCONV):
        prior = pltpu.roll(seg_rows, offset, 0)
        masks.append(jnp.where((rows >= offset) & (prior == seg_rows), 1.0, 0.0).astype(F32))
    return seg_rows, seg_cols, masks


def conv_silu(values, taps, masks):
    summed = taps[KCONV - 1 : KCONV] * values
    for offset in range(1, KCONV):
        shifted = pltpu.roll(values, offset, 0) * masks[offset - 1]
        summed = summed + taps[KCONV - 1 - offset : KCONV - offset] * shifted
    sig = sigmoid(summed)
    return summed * sig, sig * (1.0 + summed * (1.0 - sig))


def conv_back(cotangent, values, taps, masks):
    result = taps[KCONV - 1 : KCONV] * cotangent
    tap_grads = [None] * KCONV
    tap_grads[KCONV - 1] = jnp.sum(cotangent * values, axis=0, keepdims=True)
    for offset in range(1, KCONV):
        moved = pltpu.roll(cotangent * masks[offset - 1], LANES - offset, 0)
        result = result + taps[KCONV - 1 - offset : KCONV - offset] * moved
        tap_grads[KCONV - 1 - offset] = jnp.sum(moved * values, axis=0, keepdims=True)
    return result, tap_grads


def head_expander(heads):
    shape = (heads, heads * HDIM)
    return jnp.where(iota(1, shape) // HDIM == iota(0, shape), 1.0, 0.0).astype(BF16)


def two_halves(value):
    left = iota(1) < HDIM
    zero = jnp.zeros_like(value)
    return jnp.concatenate([jnp.where(left, value, zero), jnp.where(left, zero, value)], axis=0)


def staged_forward(count_ref, *refs):
    count = FORWARD_ARGS
    inputs, outputs, held, sems = refs[:count], refs[count : -count - 1], refs[-count - 1 : -1], refs[-1]
    copies = [
        pltpu.make_async_copy(source, target, sems.at[i])
        for i, (source, target) in enumerate(zip(inputs, held))
    ]
    for copy in copies:
        copy.start()
    for copy in copies:
        copy.wait()
    forward_kernel(count_ref, *held, *outputs)


def forward_kernel(
    count_ref, z_ref, x_ref, b_ref, c_ref, dt_ref, seg_ref, cx_ref, cb_ref, cc_ref, al_ref, bias_ref, skip_ref, gain_ref,
    norm_ref, xc_ref, dsx_ref, ssm_ref, gate_ref, dgate_ref, bcc_ref, small_ref, cumt_ref, rms_ref,
):
    heads = dt_ref.shape[0]
    tiles = x_ref.shape[1] // LANES
    seg_rows, seg_cols, masks = shift_masks(seg_ref[...])
    rows, cols = iota(0), iota(1)
    causal = (rows >= cols) & (seg_rows == seg_cols)

    b_conv, b_slope = conv_silu(b_ref[...].astype(F32), cb_ref[...], masks)
    c_conv, c_slope = conv_silu(c_ref[...].astype(F32), cc_ref[...], masks)
    bcc_ref[0] = b_conv
    bcc_ref[1] = c_conv
    bcc_ref[2] = b_slope
    bcc_ref[3] = c_slope
    scores = dot_nt(c_conv, b_conv)
    bcc_ref[4] = scores.T

    raw = dt_ref[...].astype(F32).T + bias_ref[...]
    step = jnp.maximum(raw, 0.0) + jnp.log1p(jnp.exp(-jnp.abs(raw)))
    decay = -jnp.exp(al_ref[...]) * step
    lower = jnp.where(rows >= cols, 1.0, 0.0).astype(BF16)
    cumul = sum(jnp.dot(lower, piece, preferred_element_type=F32) for piece in split3(decay))
    cumul_t = cumul.T
    cumt_ref[...] = cumul_t
    small_ref[0] = step
    small_ref[1] = decay
    small_ref[2] = cumul
    small_ref[3] = sigmoid(raw)

    expander = head_expander(heads)
    step_wide = dot_exact(split3(step), expander)
    skip_wide = dot_exact(split3(jnp.broadcast_to(skip_ref[...], (8, heads))), expander)

    squares = jnp.zeros((LANES, LANES), F32)
    for tile in range(tiles):
        span = slice(tile * LANES, (tile + 1) * LANES)
        x_conv, x_slope = conv_silu(x_ref[:, span].astype(F32), cx_ref[:, span], masks)
        xc_ref[:, span] = x_conv
        dsx_ref[:, span] = x_slope
        pieces = []
        for head in (2 * tile, 2 * tile + 1):
            gap = cumul[:, head : head + 1] - cumul_t[head : head + 1, :]
            pieces.append(scores * jnp.exp(jnp.where(causal, gap, -1e30)))
        weights = jnp.concatenate(pieces, axis=1)
        ssm = dot_nn(weights, two_halves(step_wide[:, span] * x_conv))
        ssm = ssm + skip_wide[0:1, span] * x_conv
        ssm_ref[:, span] = ssm
        z_tile = z_ref[:, span].astype(F32)
        sig = sigmoid(z_tile)
        gate = z_tile * sig
        gate_ref[:, span] = gate
        dgate_ref[:, span] = sig * (1.0 + z_tile * (1.0 - sig))
        gated = ssm * gate
        squares = squares + gated * gated
    mean = jnp.sum(squares, axis=1, keepdims=True) / (tiles * LANES)
    inv = lax.rsqrt(jnp.broadcast_to(mean, (LANES, LANES)) + EPS)
    rms_ref[...] = inv
    alive = jnp.where(rows < count_ref[0], 1.0, 0.0).astype(F32)
    for tile in range(tiles):
        span = slice(tile * LANES, (tile + 1) * LANES)
        normed = ssm_ref[:, span] * gate_ref[:, span] * inv * gain_ref[:, span]
        norm_ref[:, span] = (normed * alive).astype(BF16)


def backward_kernel(
    count_ref, rows_ref, w_ref, x_ref, b_ref, c_ref, seg_ref, cx_ref, cb_ref, cc_ref, al_ref, skip_ref, gain_ref,
    xc_ref, dsx_ref, ssm_ref, gate_ref, dgate_ref, bcc_ref, small_ref, cumt_ref, rms_ref,
    gz_ref, gx_ref, gb_ref, gc_ref, gdt_ref, par_ref, w_vmem, up_ref, sems,
):
    depth = w_ref.shape[0] // CHUNKS
    copies = [
        pltpu.make_async_copy(
            w_ref.at[pl.ds(i * depth, depth)], w_vmem.at[pl.ds(i * depth, depth)], sems.at[i]
        )
        for i in range(CHUNKS)
    ]
    for copy in copies:
        copy.start()
    heads = small_ref.shape[2]
    tiles = x_ref.shape[1] // LANES
    seg_rows, seg_cols, masks = shift_masks(seg_ref[...])
    rows, cols = iota(0), iota(1)
    causal_t = (cols >= rows) & (seg_rows == seg_cols)
    alive = jnp.where(rows < count_ref[0], 1.0, 0.0).astype(F32)
    inv = rms_ref[...]
    scores_t = bcc_ref[4]
    step, decay, cumul, slope = small_ref[0], small_ref[1], small_ref[2], small_ref[3]
    cumul_t = cumt_ref[...]
    expander = head_expander(heads)
    step_wide = dot_exact(split3(step), expander)
    skip_wide = dot_exact(split3(jnp.broadcast_to(skip_ref[...], (8, heads))), expander)

    place = count_ref[1]
    for i, copy in enumerate(copies):
        part = slice(i * depth, (i + 1) * depth)
        left = jnp.concatenate(
            [rows_ref[lax.bitwise_xor(place, j), :, part] for j in range(rows_ref.shape[0])], axis=0
        )
        copy.wait()
        product = jnp.dot(left, w_vmem[part, :], preferred_element_type=F32)
        up_ref[...] = product if i == 0 else up_ref[...] + product

    dots = jnp.zeros((LANES, LANES), F32)
    for tile in range(tiles):
        span = slice(tile * LANES, (tile + 1) * LANES)
        upstream = up_ref[:, span] * alive
        gated = ssm_ref[:, span] * gate_ref[:, span]
        product = upstream * gated
        dots = dots + product * gain_ref[:, span]
        par_ref[32 + tile : 33 + tile, :] = jnp.sum(product * inv, axis=0, keepdims=True)
    mean = jnp.sum(dots, axis=1, keepdims=True) / (tiles * LANES)
    pull = jnp.broadcast_to(mean, (LANES, LANES)) * inv * inv * inv

    before = jnp.where(rows > cols, 1.0, 0.0).astype(BF16)
    before = jnp.concatenate([before, before], axis=1)
    after = jnp.where(cols >= rows, 1.0, 0.0).astype(F32)
    score_grad = jnp.zeros((LANES, LANES), F32)
    sums = jnp.zeros((LANES, LANES), F32)
    for tile in range(tiles):
        span = slice(tile * LANES, (tile + 1) * LANES)
        x_conv = xc_ref[:, span]
        ssm = ssm_ref[:, span]
        gate = gate_ref[:, span]
        d_gated = inv * (up_ref[:, span] * alive) * gain_ref[:, span] - ssm * gate * pull
        gz_ref[:, span] = (d_gated * ssm * dgate_ref[:, span]).astype(BF16)
        d_ssm = d_gated * gate
        x_step = step_wide[:, span] * x_conv
        d_weights = dot_nt(two_halves(x_step), d_ssm)
        pieces = []
        for which in range(2):
            head = 2 * tile + which
            gap = cumul_t[head : head + 1, :] - cumul[:, head : head + 1]
            fade = jnp.exp(jnp.where(causal_t, gap, -1e30))
            d_weight = d_weights[which * LANES : (which + 1) * LANES, :] * fade
            score_grad = score_grad + d_weight
            pieces.append((scores_t * fade, d_weight * scores_t))
        d_xstep = dot_nn(
            jnp.concatenate([pieces[0][0], pieces[1][0]], axis=1), two_halves(d_ssm)
        )
        gaps_h, gaps_l = split2(jnp.concatenate([pieces[0][1], pieces[1][1]], axis=1))
        gaps = jnp.dot(
            before, jnp.concatenate([gaps_h, gaps_l], axis=0), preferred_element_type=F32
        )
        terms = (
            gaps[:, :LANES] * after,
            gaps[:, LANES:] * after,
            d_xstep * x_conv,
            d_ssm * x_conv,
        )
        pickers = (
            jnp.where(cols == 2 * tile, 1.0, 0.0),
            jnp.where(cols == 2 * tile + 1, 1.0, 0.0),
            jnp.where(cols == heads + 2 * tile + rows // HDIM, 1.0, 0.0),
            jnp.where(cols == 2 * heads + 2 * tile + rows // HDIM, 1.0, 0.0),
        )
        left, right = [], []
        for term, picker in zip(terms, pickers):
            term_h, term_l = split2(term)
            left += [term_h, term_l]
            right += [picker.astype(BF16)] * 2
        sums = sums + jnp.dot(
            jnp.concatenate(left, axis=1),
            jnp.concatenate(right, axis=0),
            preferred_element_type=F32,
        )
        d_conv = skip_wide[0:1, span] * d_ssm + step_wide[:, span] * d_xstep
        x_grad, tap_grads = conv_back(
            d_conv * dsx_ref[:, span], x_ref[:, span].astype(F32), cx_ref[:, span], masks
        )
        gx_ref[:, span] = x_grad.astype(BF16)
        for tap in range(KCONV):
            par_ref[tap * tiles + tile : tap * tiles + tile + 1, :] = tap_grads[tap]

    d_decay = sums[:, 0:heads]
    d_step = sums[:, heads : 2 * heads] - jnp.exp(al_ref[...]) * d_decay
    d_raw = d_step * slope
    gdt_ref[...] = d_raw.T.astype(BF16)
    par_ref[48:49, 0:heads] = jnp.sum(d_decay * decay, axis=0, keepdims=True)
    par_ref[49:50, 0:heads] = jnp.sum(d_raw, axis=0, keepdims=True)
    par_ref[50:51, 0:heads] = jnp.sum(sums[:, 2 * heads : 3 * heads], axis=0, keepdims=True)

    b_conv, c_conv = bcc_ref[0], bcc_ref[1]
    b_grad, tap_grads = conv_back(
        dot_nn(score_grad, c_conv) * bcc_ref[2], b_ref[...].astype(F32), cb_ref[...], masks
    )
    gb_ref[...] = b_grad.astype(BF16)
    for tap in range(KCONV):
        par_ref[40 + tap : 41 + tap, :] = tap_grads[tap]
    c_grad, tap_grads = conv_back(
        dot_nn(score_grad.T, b_conv) * bcc_ref[3], c_ref[...].astype(F32), cc_ref[...], masks
    )
    gc_ref[...] = c_grad.astype(BF16)
    for tap in range(KCONV):
        par_ref[44 + tap : 45 + tap, :] = tap_grads[tap]


def unpack_kernel(par_ref, cx_ref, cb_ref, cc_ref, al_ref, bias_ref, skip_ref, gain_ref):
    heads = al_ref.shape[1]
    tiles = cx_ref.shape[1] // LANES
    total = par_ref[...]
    for tap in range(KCONV):
        for tile in range(tiles):
            cx_ref[tap : tap + 1, tile * LANES : (tile + 1) * LANES] = total[
                tap * tiles + tile : tap * tiles + tile + 1
            ]
    for tile in range(tiles):
        gain_ref[:, tile * LANES : (tile + 1) * LANES] = total[32 + tile : 33 + tile]
    cb_ref[...] = total[40:44]
    cc_ref[...] = total[44:48]
    al_ref[...] = total[48:49, 0:heads]
    bias_ref[...] = total[49:50, 0:heads]
    skip_ref[...] = total[50:51, 0:heads]


def weight_kernel(meta_ref, col_ref, own_ref, *refs):
    *blocks, out_ref = refs
    place, chip, core = meta_ref[1], meta_ref[2], meta_ref[3]
    chips = col_ref.shape[0] // 2
    reach = chips // 2

    def columns(shard):
        return [col_ref[shard, lax.bitwise_xor(place, j)] for j in range(col_ref.shape[1])]

    def product(pieces, block):
        return lax.dot_general(
            jnp.concatenate(pieces, axis=0), block, (((0,), (0,)), ((), ())), preferred_element_type=F32
        )

    def pair(which):
        return columns(2 * which) + columns(2 * which + 1)

    total = product(pair(chip), own_ref[...])
    toward = 1 - 2 * core
    for k in range(1, reach):
        back = lax.rem(chip - toward * k + chips, chips)
        ahead = lax.rem(chip + toward * k + chips, chips)
        total = total + product(pair(back), blocks[k - 1][...])
        total = total + product(pair(ahead), blocks[reach + k - 1][...])
    far = 2 * lax.rem(chip + reach, chips)
    total = total + product(columns(far + core), blocks[reach - 1][...])
    total = total + product(columns(far + 1 - core), blocks[2 * reach - 1][...])
    out_ref[...] = total.astype(out_ref.dtype)


def call(kernel, operands, outs, flops, smem=1, hbm=(), scratch=(), fixed=(), limit=32):
    vmem = pl.BlockSpec(memory_space=pltpu.VMEM)
    specs = [pl.BlockSpec()] * len(operands)
    for i in range(smem):
        specs[i] = pl.BlockSpec(memory_space=pltpu.SMEM)
    for i in hbm:
        specs[i] = pl.BlockSpec(memory_space=pl.ANY)
    for i in fixed:
        specs[i] = vmem
    size = sum(a.size * a.dtype.itemsize for a in operands) + sum(
        a.size * a.dtype.itemsize for a in outs
    )
    return pl.pallas_call(
        kernel,
        out_shape=outs,
        in_specs=specs,
        out_specs=[vmem] * len(outs),
        scratch_shapes=scratch,
        compiler_params=pltpu.CompilerParams(vmem_limit_bytes=limit * MIB),
        cost_estimate=pl.CostEstimate(flops=flops, bytes_accessed=size, transcendentals=0),
    )(*operands)


def shape(dims, dtype=F32):
    return jax.ShapeDtypeStruct(dims, dtype)


def swap(value, axis, bit, size):
    return lax.ppermute(value, axis, [(i, i ^ bit) for i in range(size)])


def gather_tensor(block, axis):
    held = jnp.expand_dims(block, (axis, axis + 1, axis + 2))
    for bit, where in ((4, axis), (1, axis + 2), (2, axis + 1)):
        held = jnp.concatenate([held, swap(held, "tensor", bit, 8)], axis=where)
    return held.reshape(block.shape[:axis] + (8,) + block.shape[axis:])


def gather_chips(block, core, dp):
    chips, size = dp // 2, block.shape[0]
    other = swap(block, "dp", 1, dp)
    first = core == 0
    pair = jnp.concatenate([jnp.where(first, block, other), jnp.where(first, other, block)], axis=0)
    ring = [(2 * z, 2 * ((z + 1) % chips)) for z in range(chips)]
    ring += [(2 * z + 1, 2 * ((z - 1) % chips) + 1) for z in range(chips)]
    got, current = [], pair
    for _ in range(chips // 2 - 1):
        current = lax.ppermute(current, "dp", ring)
        got.append(current)
    got.append(lax.ppermute(jnp.where(first, current[:size], current[size:]), "dp", ring))
    return pair, *got, *[swap(value, "dp", 1, dp) for value in got]


def body(
    z_act, x_act, b_act, c_act, dt_act, segment, counts,
    conv_x, conv_b, conv_c, a_log, dt_bias, d_skip, norm_gain, w_out, d_out,
):
    length, width = z_act.shape
    heads = dt_act.shape[1]
    own, features = d_out.shape
    dp = lax.axis_size("dp")
    shard = lax.axis_index("dp")
    core = shard % 2
    meta = jnp.stack([counts[0], lax.axis_index("tensor"), shard // 2, core]).astype(jnp.int32)
    seg_row = segment.reshape(1, length)
    a_log, dt_bias, d_skip = (v.reshape(1, heads) for v in (a_log, dt_bias, d_skip))
    gain = norm_gain.reshape(1, width)

    w_all = lax.all_gather(w_out, "dp", axis=0, tiled=True)

    rows = gather_tensor(d_out, 0)
    pieces = d_out.reshape(own, dp, features // dp).transpose(1, 0, 2)
    pieces = lax.all_to_all(pieces, "dp", 0, 0, tiled=False)
    columns = gather_tensor(pieces, 1)

    wide = shape((length, width))
    operands = (
        meta, z_act, x_act, b_act, c_act, dt_act.T, seg_row, conv_x, conv_b, conv_c, a_log, dt_bias, d_skip, gain,
    )
    normed, *saved = call(
        staged_forward,
        operands,
        [
            shape((length, width), BF16), wide, wide, wide, wide, wide,
            shape((5, LANES, LANES)), shape((4, length, heads)), shape((heads, length)), shape((LANES, LANES)),
        ],
        300_000_000,
        hbm=range(1, 1 + FORWARD_ARGS),
        limit=56,
        scratch=[pltpu.VMEM(a.shape, a.dtype) for a in operands[1:]] + [pltpu.SemaphoreType.DMA((FORWARD_ARGS,))],
    )
    blocks = gather_chips(normed, core, dp)

    operands = (
        meta, rows, w_all, x_act, b_act, c_act, seg_row, conv_x, conv_b, conv_c, a_log, d_skip, gain, *saved,
    )
    *act_grads, packed = call(
        backward_kernel,
        operands,
        [
            shape((length, width), BF16), shape((length, width), BF16), shape((length, LANES), BF16),
            shape((length, LANES), BF16), shape((heads, length), BF16), shape((56, LANES)),
        ],
        1_700_000_000,
        hbm=(2,),
        fixed=(1, *range(len(operands) - len(saved), len(operands))),
        scratch=[
            pltpu.VMEM((features, width), BF16), pltpu.VMEM((length, width), F32), pltpu.SemaphoreType.DMA((CHUNKS,)),
        ],
    )
    act_grads[4] = act_grads[4].T
    packed = packed + swap(packed, "dp", 1, dp)
    packed = packed + swap(packed, "rep", 1, 2)
    for bit in (2, 4, 8):
        packed = packed + swap(packed, "dp", bit, dp)
    sums = call(
        unpack_kernel,
        (packed,),
        [
            shape(conv_x.shape), shape(conv_b.shape), shape(conv_c.shape),
            shape((1, heads)), shape((1, heads)), shape((1, heads)), shape((1, width)),
        ],
        1000,
        smem=0,
    )

    share = call(
        weight_kernel,
        (meta, columns, *blocks),
        [shape((features // dp, width), BF16)],
        1_100_000_000,
        fixed=range(1, 2 + len(blocks)),
    )[0]
    weight_grad = share.astype(F32) + swap(share, "rep", 1, 2).astype(F32)
    return (
        *act_grads,
        sums[0], sums[1], sums[2],
        sums[3].reshape(heads), sums[4].reshape(heads), sums[5].reshape(heads), sums[6].reshape(width),
        weight_grad,
    )


def solution(mesh):
    tokens = P(("rep", "dp"), "tensor")
    shards = P(("rep", "dp"))
    taps = P(None, "tensor")
    per_head = P("tensor")
    weight = P("dp", "tensor")
    in_specs = (
        *([tokens] * 5), shards, shards, *([taps] * 3), *([per_head] * 4),
        weight, P(("rep", "dp", "tensor"), None),
    )
    out_specs = (*([tokens] * 5), *([taps] * 3), *([per_head] * 4), weight)
    return jax.shard_map(body, mesh=mesh, in_specs=in_specs, out_specs=out_specs, check_vma=False)
```

```python
import jax
import jax.numpy as jnp
from jax import lax
from jax.experimental import pallas as pl
from jax.experimental.pallas import tpu as pltpu
from jax.sharding import PartitionSpec as P

HDIM = 64
LANES = 128
KCONV = 4
EPS = 1e-05
F32 = jnp.float32
BF16 = jnp.bfloat16
VMEM_LIMIT = 56 * 1024 * 1024
SHARDS = 16
PIECES = ((0, 0), (0, 1), (3, 0), (3, 1), (1, 0), (1, 1), (2, 0), (2, 1))


def split2(value):
    high = value.astype(BF16)
    low = (value - high.astype(F32)).astype(BF16)
    return high, low


def split3(value):
    high = value.astype(BF16)
    rest = value - high.astype(F32)
    middle = rest.astype(BF16)
    low = (rest - middle.astype(F32)).astype(BF16)
    return high, middle, low


def dot_nn(left, right):
    left_h, left_l = split2(left)
    right_h, right_l = split2(right)
    return jnp.dot(
        jnp.concatenate([left_h, left_h, left_l], axis=1),
        jnp.concatenate([right_h, right_l, right_h], axis=0),
        preferred_element_type=F32,
    )


def dot_nt(left, right):
    left_h, left_l = split2(left)
    right_h, right_l = split2(right)
    return lax.dot_general(
        jnp.concatenate([left_h, left_h, left_l], axis=1),
        jnp.concatenate([right_h, right_l, right_h], axis=1),
        (((1,), (1,)), ((), ())),
        preferred_element_type=F32,
    )


def dot_exact(left_pieces, right):
    total = jnp.dot(left_pieces[0], right, preferred_element_type=F32)
    for piece in left_pieces[1:]:
        total = total + jnp.dot(piece, right, preferred_element_type=F32)
    return total


def sigmoid(value):
    return 1.0 / (1.0 + jnp.exp(-value))


def iota(axis, shape=(LANES, LANES)):
    return lax.broadcasted_iota(jnp.int32, shape, axis)


def shift_masks(seg_row):
    seg_cols = jnp.broadcast_to(seg_row.astype(F32), (LANES, LANES))
    seg_rows = seg_cols.T
    rows = iota(0)
    masks = []
    for offset in range(1, KCONV):
        prior = pltpu.roll(seg_rows, offset, 0)
        masks.append(jnp.where((rows >= offset) & (prior == seg_rows), 1.0, 0.0).astype(F32))
    return seg_rows, seg_cols, masks


def conv_silu(values, taps, masks):
    summed = taps[KCONV - 1 : KCONV] * values
    for offset in range(1, KCONV):
        shifted = pltpu.roll(values, offset, 0) * masks[offset - 1]
        summed = summed + taps[KCONV - 1 - offset : KCONV - offset] * shifted
    sig = sigmoid(summed)
    return summed * sig, sig * (1.0 + summed * (1.0 - sig))


def conv_back(cotangent, values, taps, masks):
    result = taps[KCONV - 1 : KCONV] * cotangent
    tap_grads = [None] * KCONV
    tap_grads[KCONV - 1] = jnp.sum(cotangent * values, axis=0, keepdims=True)
    for offset in range(1, KCONV):
        moved = pltpu.roll(cotangent * masks[offset - 1], LANES - offset, 0)
        result = result + taps[KCONV - 1 - offset : KCONV - offset] * moved
        tap_grads[KCONV - 1 - offset] = jnp.sum(moved * values, axis=0, keepdims=True)
    return result, tap_grads


def head_expander(heads):
    shape = (heads, heads * HDIM)
    return jnp.where(iota(1, shape) // HDIM == iota(0, shape), 1.0, 0.0).astype(BF16)


def two_halves(value):
    left = iota(1) < HDIM
    zero = jnp.zeros_like(value)
    return jnp.concatenate([jnp.where(left, value, zero), jnp.where(left, zero, value)], axis=0)


def picked(dims, half):
    axis = len(dims) - 4 if len(dims) > 3 else 0
    span = dims[axis] // 2
    return (slice(None),) * axis + (pl.ds(half * span, span),), (*dims[:axis], span, *dims[axis + 1 :])


def staged(kernel, count, half):
    def run(meta_ref, *refs):
        inputs, rest = refs[:count], refs[count:]
        outputs, held, sems = rest[: -count - 1], rest[-count - 1 : -1], rest[-1]
        copies = []
        for i, (source, target) in enumerate(zip(inputs, held)):
            if half is not None:
                source = source.at[picked(source.shape, half)[0]]
            copies.append(pltpu.make_async_copy(source, target, sems.at[i]))
        for copy in copies:
            copy.start()
        if half is not None:
            kernel(meta_ref, copies, *held, *outputs)
        else:
            wait(copies)
            kernel(meta_ref, *held, *outputs)

    return run


def wait(copies):
    for copy in copies:
        copy.wait()


def place_pieces(meta_ref, refs, target):
    near, up, down, far0, far1 = refs
    pieces = [near.at[0], near.at[1], up.at[0], up.at[1], down.at[0], down.at[1], far0, far1]
    along, across = meta_ref[1], meta_ref[2]
    for piece, (far_x, far_y) in zip(pieces, PIECES):
        index = lax.rem(along + far_x, 4) * 2 + lax.bitwise_xor(across, far_y)
        target[:, :, pl.ds(pl.multiple_of(index * 16, 16), 16), :] = piece[...]


def forward_kernel(
    count_ref, z_ref, x_ref, b_ref, c_ref, dt_ref, seg_ref, cx_ref, cb_ref, cc_ref, al_ref, bias_ref, skip_ref, gain_ref,
    norm_ref, xc_ref, dsx_ref, ssm_ref, gate_ref, dgate_ref, bcc_ref, small_ref, cumt_ref, rms_ref,
):
    heads = dt_ref.shape[0]
    tiles = x_ref.shape[1] // LANES
    seg_rows, seg_cols, masks = shift_masks(seg_ref[...])
    rows, cols = iota(0), iota(1)
    causal = (rows >= cols) & (seg_rows == seg_cols)

    b_conv, b_slope = conv_silu(b_ref[...].astype(F32), cb_ref[...], masks)
    c_conv, c_slope = conv_silu(c_ref[...].astype(F32), cc_ref[...], masks)
    bcc_ref[0] = b_conv
    bcc_ref[1] = c_conv
    bcc_ref[2] = b_slope
    bcc_ref[3] = c_slope
    scores = dot_nt(c_conv, b_conv)
    bcc_ref[4] = scores.T

    raw = dt_ref[...].astype(F32).T + bias_ref[...]
    step = jnp.maximum(raw, 0.0) + jnp.log1p(jnp.exp(-jnp.abs(raw)))
    decay = -jnp.exp(al_ref[...]) * step
    lower = jnp.where(rows >= cols, 1.0, 0.0).astype(BF16)
    cumul = sum(jnp.dot(lower, piece, preferred_element_type=F32) for piece in split3(decay))
    cumul_t = cumul.T
    cumt_ref[...] = cumul_t
    small_ref[0] = step
    small_ref[1] = decay
    small_ref[2] = cumul
    small_ref[3] = sigmoid(raw)

    expander = head_expander(heads)
    step_wide = dot_exact(split3(step), expander)
    skip_wide = dot_exact(split3(jnp.broadcast_to(skip_ref[...], (8, heads))), expander)

    squares = jnp.zeros((LANES, LANES), F32)
    for tile in range(tiles):
        span = slice(tile * LANES, (tile + 1) * LANES)
        x_conv, x_slope = conv_silu(x_ref[:, span].astype(F32), cx_ref[:, span], masks)
        xc_ref[:, span] = x_conv
        dsx_ref[:, span] = x_slope
        pieces = []
        for head in (2 * tile, 2 * tile + 1):
            gap = cumul[:, head : head + 1] - cumul_t[head : head + 1, :]
            pieces.append(scores * jnp.exp(jnp.where(causal, gap, -1e30)))
        weights = jnp.concatenate(pieces, axis=1)
        ssm = dot_nn(weights, two_halves(step_wide[:, span] * x_conv))
        ssm = ssm + skip_wide[0:1, span] * x_conv
        ssm_ref[:, span] = ssm
        z_tile = z_ref[:, span].astype(F32)
        sig = sigmoid(z_tile)
        gate = z_tile * sig
        gate_ref[:, span] = gate
        dgate_ref[:, span] = sig * (1.0 + z_tile * (1.0 - sig))
        gated = ssm * gate
        squares = squares + gated * gated
    mean = jnp.sum(squares, axis=1, keepdims=True) / (tiles * LANES)
    inv = lax.rsqrt(jnp.broadcast_to(mean, (LANES, LANES)) + EPS)
    rms_ref[...] = inv
    alive = jnp.where(rows < count_ref[0], 1.0, 0.0).astype(F32)
    for tile in range(tiles):
        span = slice(tile * LANES, (tile + 1) * LANES)
        normed = ssm_ref[:, span] * gate_ref[:, span] * inv * gain_ref[:, span]
        norm_ref[:, span] = (normed * alive).astype(BF16)


def upstream_kernel(meta_ref, copies, near, up, down, far0, far1, *refs):
    *weights, own_ref, other_ref, rows_ref, sum_ref = refs
    wait(copies[:5])
    place_pieces(meta_ref, (near, up, down, far0, far1), rows_ref)
    order = ring_order(meta_ref)
    for i in range(0, len(weights), 2):
        wait(copies[5 + i : 7 + i])
        left = [
            jnp.concatenate([rows_ref[who, order[i]], rows_ref[who, order[i + 1]]], axis=1) for who in range(2)
        ]
        product = jnp.dot(
            jnp.concatenate(left, axis=0),
            jnp.concatenate([weights[i][...], weights[i + 1][...]], axis=0),
            preferred_element_type=F32,
        )
        sum_ref[...] = product if i == 0 else sum_ref[...] + product
    length = own_ref.shape[0]
    own_ref[...] = sum_ref[:length, :]
    other_ref[...] = sum_ref[length:, :].astype(BF16)


def backward_kernel(meta_ref, own_ref, other_ref, *refs):
    *rest, up_ref = refs
    up_ref[...] = own_ref[...] + other_ref[...].astype(F32)
    pull_back(meta_ref, up_ref, *rest)


def ring_order(meta_ref):
    chip, core = meta_ref[3], meta_ref[4]
    other = 1 - core
    toward = 1 - 2 * core
    order = [2 * chip + core, 2 * chip + other]
    for k in (1, 2, 3):
        back = 2 * lax.rem(chip - toward * k + 8, 8)
        ahead = 2 * lax.rem(chip + toward * k + 8, 8)
        order += [back + core, back + other, ahead + other, ahead + core]
    far = 2 * lax.rem(chip + 4, 8)
    return order + [far + core, far + other]


def pull_back(
    count_ref, up_ref, x_ref, b_ref, c_ref, seg_ref, cx_ref, cb_ref, cc_ref, al_ref, skip_ref, gain_ref,
    xc_ref, dsx_ref, ssm_ref, gate_ref, dgate_ref, bcc_ref, small_ref, cumt_ref, rms_ref,
    gz_ref, gx_ref, gb_ref, gc_ref, gdt_ref, par_ref,
):
    heads = small_ref.shape[2]
    tiles = x_ref.shape[1] // LANES
    seg_rows, seg_cols, masks = shift_masks(seg_ref[...])
    rows, cols = iota(0), iota(1)
    causal_t = (cols >= rows) & (seg_rows == seg_cols)
    alive = jnp.where(rows < count_ref[0], 1.0, 0.0).astype(F32)
    inv = rms_ref[...]
    scores_t = bcc_ref[4]
    step, decay, cumul, slope = small_ref[0], small_ref[1], small_ref[2], small_ref[3]
    cumul_t = cumt_ref[...]
    expander = head_expander(heads)
    step_wide = dot_exact(split3(step), expander)
    skip_wide = dot_exact(split3(jnp.broadcast_to(skip_ref[...], (8, heads))), expander)

    dots = jnp.zeros((LANES, LANES), F32)
    for tile in range(tiles):
        span = slice(tile * LANES, (tile + 1) * LANES)
        upstream = up_ref[:, span] * alive
        gated = ssm_ref[:, span] * gate_ref[:, span]
        product = upstream * gated
        dots = dots + product * gain_ref[:, span]
        par_ref[32 + tile : 33 + tile, :] = jnp.sum(product * inv, axis=0, keepdims=True)
    mean = jnp.sum(dots, axis=1, keepdims=True) / (tiles * LANES)
    pull = jnp.broadcast_to(mean, (LANES, LANES)) * inv * inv * inv

    before = jnp.where(rows > cols, 1.0, 0.0).astype(BF16)
    before = jnp.concatenate([before, before], axis=1)
    after = jnp.where(cols >= rows, 1.0, 0.0).astype(F32)
    score_grad = jnp.zeros((LANES, LANES), F32)
    sums = jnp.zeros((LANES, LANES), F32)
    for tile in range(tiles):
        span = slice(tile * LANES, (tile + 1) * LANES)
        x_conv = xc_ref[:, span]
        ssm = ssm_ref[:, span]
        gate = gate_ref[:, span]
        d_gated = inv * (up_ref[:, span] * alive) * gain_ref[:, span] - ssm * gate * pull
        gz_ref[:, span] = (d_gated * ssm * dgate_ref[:, span]).astype(BF16)
        d_ssm = d_gated * gate
        x_step = step_wide[:, span] * x_conv
        d_weights = dot_nt(two_halves(x_step), d_ssm)
        pieces = []
        for which in range(2):
            head = 2 * tile + which
            gap = cumul_t[head : head + 1, :] - cumul[:, head : head + 1]
            fade = jnp.exp(jnp.where(causal_t, gap, -1e30))
            d_weight = d_weights[which * LANES : (which + 1) * LANES, :] * fade
            score_grad = score_grad + d_weight
            pieces.append((scores_t * fade, d_weight * scores_t))
        d_xstep = dot_nn(
            jnp.concatenate([pieces[0][0], pieces[1][0]], axis=1), two_halves(d_ssm)
        )
        gaps_h, gaps_l = split2(jnp.concatenate([pieces[0][1], pieces[1][1]], axis=1))
        gaps = jnp.dot(
            before, jnp.concatenate([gaps_h, gaps_l], axis=0), preferred_element_type=F32
        )
        terms = (
            gaps[:, :LANES] * after,
            gaps[:, LANES:] * after,
            d_xstep * x_conv,
            d_ssm * x_conv,
        )
        pickers = (
            jnp.where(cols == 2 * tile, 1.0, 0.0),
            jnp.where(cols == 2 * tile + 1, 1.0, 0.0),
            jnp.where(cols == heads + 2 * tile + rows // HDIM, 1.0, 0.0),
            jnp.where(cols == 2 * heads + 2 * tile + rows // HDIM, 1.0, 0.0),
        )
        left, right = [], []
        for term, picker in zip(terms, pickers):
            term_h, term_l = split2(term)
            left += [term_h, term_l]
            right += [picker.astype(BF16)] * 2
        sums = sums + jnp.dot(
            jnp.concatenate(left, axis=1),
            jnp.concatenate(right, axis=0),
            preferred_element_type=F32,
        )
        d_conv = skip_wide[0:1, span] * d_ssm + step_wide[:, span] * d_xstep
        x_grad, tap_grads = conv_back(
            d_conv * dsx_ref[:, span], x_ref[:, span].astype(F32), cx_ref[:, span], masks
        )
        gx_ref[:, span] = x_grad.astype(BF16)
        for tap in range(KCONV):
            par_ref[tap * tiles + tile : tap * tiles + tile + 1, :] = tap_grads[tap]

    d_decay = sums[:, 0:heads]
    d_step = sums[:, heads : 2 * heads] - jnp.exp(al_ref[...]) * d_decay
    d_raw = d_step * slope
    gdt_ref[...] = d_raw.T.astype(BF16)
    par_ref[48:49, 0:heads] = jnp.sum(d_decay * decay, axis=0, keepdims=True)
    par_ref[49:50, 0:heads] = jnp.sum(d_raw, axis=0, keepdims=True)
    par_ref[50:51, 0:heads] = jnp.sum(sums[:, 2 * heads : 3 * heads], axis=0, keepdims=True)

    b_conv, c_conv = bcc_ref[0], bcc_ref[1]
    b_grad, tap_grads = conv_back(
        dot_nn(score_grad, c_conv) * bcc_ref[2], b_ref[...].astype(F32), cb_ref[...], masks
    )
    gb_ref[...] = b_grad.astype(BF16)
    for tap in range(KCONV):
        par_ref[40 + tap : 41 + tap, :] = tap_grads[tap]
    c_grad, tap_grads = conv_back(
        dot_nn(score_grad.T, b_conv) * bcc_ref[3], c_ref[...].astype(F32), cc_ref[...], masks
    )
    gc_ref[...] = c_grad.astype(BF16)
    for tap in range(KCONV):
        par_ref[44 + tap : 45 + tap, :] = tap_grads[tap]


def unpack_kernel(par_ref, cx_ref, cb_ref, cc_ref, al_ref, bias_ref, skip_ref, gain_ref):
    heads = al_ref.shape[1]
    tiles = cx_ref.shape[1] // LANES
    total = par_ref[...]
    for tap in range(KCONV):
        for tile in range(tiles):
            cx_ref[tap : tap + 1, tile * LANES : (tile + 1) * LANES] = total[
                tap * tiles + tile : tap * tiles + tile + 1
            ]
    for tile in range(tiles):
        gain_ref[:, tile * LANES : (tile + 1) * LANES] = total[32 + tile : 33 + tile]
    cb_ref[...] = total[40:44]
    cc_ref[...] = total[44:48]
    al_ref[...] = total[48:49, 0:heads]
    bias_ref[...] = total[49:50, 0:heads]
    skip_ref[...] = total[50:51, 0:heads]


def weight_kernel(meta_ref, copies, near, up, down, far0, far1, *refs):
    *blocks, out_ref, col_ref = refs
    wait(copies[:5])
    place_pieces(meta_ref, (near, up, down, far0, far1), col_ref)
    order = ring_order(meta_ref)
    total = None
    for i in range(0, len(blocks), 2):
        wait(copies[5 + i : 7 + i])
        product = lax.dot_general(
            jnp.concatenate(
                [jnp.concatenate([col_ref[0, k], col_ref[1, k]], axis=1) for k in order[i : i + 2]], axis=0
            ),
            jnp.concatenate([blocks[i][...], blocks[i + 1][...]], axis=0),
            (((0,), (0,)), ((), ())),
            preferred_element_type=F32,
        )
        total = product if i == 0 else total + product
    out_ref[...] = total.astype(out_ref.dtype)


def call(kernel, operands, outs, flops, scratch=(), half=None):
    others = operands[1:]
    size = sum(a.size * a.dtype.itemsize for a in operands) + sum(
        a.size * a.dtype.itemsize for a in outs
    )
    held = [a.shape if half is None else picked(a.shape, half)[1] for a in others]
    return pl.pallas_call(
        staged(kernel, len(others), half),
        out_shape=outs,
        in_specs=[pl.BlockSpec(memory_space=pltpu.SMEM)] + [pl.BlockSpec(memory_space=pl.ANY)] * len(others),
        out_specs=[pl.BlockSpec(memory_space=pltpu.VMEM)] * len(outs),
        scratch_shapes=[
            *scratch,
            *[pltpu.VMEM(dims, a.dtype) for dims, a in zip(held, others)],
            pltpu.SemaphoreType.DMA((len(others),)),
        ],
        compiler_params=pltpu.CompilerParams(vmem_limit_bytes=VMEM_LIMIT),
        cost_estimate=pl.CostEstimate(flops=flops, bytes_accessed=size, transcendentals=0),
    )(*operands)


def unpack(packed, outs):
    vmem = pl.BlockSpec(memory_space=pltpu.VMEM)
    return pl.pallas_call(
        unpack_kernel, out_shape=outs, in_specs=[vmem], out_specs=[vmem] * len(outs)
    )(packed)


def shape(dims, dtype=F32):
    return jax.ShapeDtypeStruct(dims, dtype)


def swap(value, axis, bit, size):
    return lax.ppermute(value, axis, [(i, i ^ bit) for i in range(size)])


def along_x(value, by):
    return lax.ppermute(value, "tensor", [(i, (i + 2 * by) % 8) for i in range(8)])


def gather_near(block):
    return jnp.stack([block, swap(block, "tensor", 1, 8)])


def gather_next(near):
    return along_x(near, 1), along_x(near, -1)


def gather_far(up, down):
    return along_x(up[0], 1), along_x(down[1], -1)


def tie(*values):
    return lax.optimization_barrier(values)


def body(
    z_act, x_act, b_act, c_act, dt_act, segment, counts,
    conv_x, conv_b, conv_c, a_log, dt_bias, d_skip, norm_gain, w_out, d_out,
):
    length, width = z_act.shape
    heads = dt_act.shape[1]
    own, features = d_out.shape
    dp = lax.axis_size("dp")
    shard = lax.axis_index("dp")
    place = lax.axis_index("tensor")
    core = lax.bitwise_and(shard, 1)
    meta = jnp.stack(
        [counts[0], lax.shift_right_logical(place, 1), lax.bitwise_and(place, 1), lax.shift_right_logical(shard, 1), core]
    )
    chips = dp // 2
    ring = [(2 * z, 2 * ((z + 1) % chips)) for z in range(chips)]
    ring += [(2 * z + 1, 2 * ((z - 1) % chips) + 1) for z in range(chips)]
    seg_row = segment.reshape(1, length)
    a_log, dt_bias, d_skip = (v.reshape(1, heads) for v in (a_log, dt_bias, d_skip))
    gain = norm_gain.reshape(1, width)
    replica = lax.axis_index("rep")
    lower = replica == 0
    half = w_out.shape[0] // 2
    w_half = jnp.where(lower, w_out[:half], w_out[half:])
    pieces = d_out.reshape(own, dp, 2, half).transpose(2, 1, 0, 3)
    theirs = swap(jnp.where(lower, pieces[1], pieces[0]), "rep", 1, 2)
    mine = jnp.where(lower, pieces[0], pieces[1])
    turned = lax.all_to_all(pieces, "dp", 1, 1, tiled=False)
    pieces = jnp.concatenate([mine[None], theirs[None], turned], axis=0)

    def step(value):
        return lax.ppermute(value, "dp", ring)

    def across(*values):
        return [swap(value, "dp", 1, dp) for value in values]

    wide = shape((length, width))
    normed, *saved = call(
        forward_kernel,
        (meta, z_act, x_act, b_act, c_act, dt_act.T, seg_row, conv_x, conv_b, conv_c, a_log, dt_bias, d_skip, gain),
        [
            shape((length, width), BF16), wide, wide, wide, wide, wide,
            shape((5, LANES, LANES)), shape((4, length, heads)), shape((heads, length)), shape((LANES, LANES)),
        ],
        5_000_000_000,
    )
    one = jnp.concatenate([w_half, normed], axis=0)
    (two,) = across(one)
    blocks = [one, two]
    one, two = step(one), step(two)
    near = gather_near(pieces)

    blocks += [one, two, *across(one, two)]
    one, two = step(one), step(two)
    up, down = gather_next(near)

    blocks += [one, two, *across(one, two)]
    one, two = step(one), step(two)
    far = gather_far(up, down)
    blocks += [one, two, *across(one, two)]
    one = step(one)
    blocks += [one, *across(one)]

    upstream, other = call(
        upstream_kernel,
        (meta, near, up, down, *far, *blocks),
        [shape((length, width)), shape((length, width), BF16)],
        4_000_000_000,
        half=0,
        scratch=[pltpu.VMEM((2, dp, length, half), BF16), pltpu.VMEM((2 * length, width), F32)],
    )
    other = swap(other, "rep", 1, 2)
    *act_grads, packed = call(
        backward_kernel,
        (
            meta, upstream, other,
            x_act, b_act, c_act, seg_row, conv_x, conv_b, conv_c, a_log, d_skip, gain, *saved,
        ),
        [
            shape((length, width), BF16), shape((length, width), BF16), shape((length, LANES), BF16),
            shape((length, LANES), BF16), shape((heads, length), BF16), shape((56, LANES)),
        ],
        10_000_000_000,
        scratch=[pltpu.VMEM((length, width), F32)],
    )
    act_grads[4] = act_grads[4].T
    share = call(
        weight_kernel,
        (meta, near, up, down, *far, *blocks),
        [shape((features // dp, width), BF16)],
        5_000_000_000,
        half=1,
        scratch=[pltpu.VMEM((2, dp, length, half), BF16)],
    )[0]
    weight_grad = share.astype(F32) + swap(share, "rep", 1, 2).astype(F32)
    for bit in (1, 2, 4):
        packed = packed + swap(packed, "dp", bit, dp)
    packed = packed + swap(packed, "rep", 1, 2)
    packed = packed + swap(packed, "dp", 8, dp)
    sums = unpack(
        packed,
        [
            shape(conv_x.shape), shape(conv_b.shape), shape(conv_c.shape),
            shape((1, heads)), shape((1, heads)), shape((1, heads)), shape((1, width)),
        ],
    )

    return (
        *act_grads,
        sums[0], sums[1], sums[2],
        sums[3].reshape(heads), sums[4].reshape(heads), sums[5].reshape(heads), sums[6].reshape(width),
        weight_grad,
    )


def solution(mesh):
    tokens = P(("rep", "dp"), "tensor")
    shards = P(("rep", "dp"))
    taps = P(None, "tensor")
    per_head = P("tensor")
    weight = P("dp", "tensor")
    in_specs = (
        *([tokens] * 5), shards, shards, *([taps] * 3), *([per_head] * 4),
        weight, P(("rep", "dp", "tensor"), None),
    )
    out_specs = (*([tokens] * 5), *([taps] * 3), *([per_head] * 4), weight)
    return jax.shard_map(body, mesh=mesh, in_specs=in_specs, out_specs=out_specs, check_vma=False)
```

```python
import jax
import jax.numpy as jnp
from jax import lax
from jax.experimental import pallas as pl
from jax.experimental.pallas import tpu as pltpu
from jax.sharding import PartitionSpec as P

HDIM = 64
LANES = 128
KCONV = 4
EPS = 1e-05
F32 = jnp.float32
BF16 = jnp.bfloat16
VMEM_LIMIT = 56 * 1024 * 1024
SHARDS = 16
PIECES = ((0, 0), (0, 1), (3, 0), (3, 1), (1, 0), (1, 1), (2, 0), (2, 1))


def split2(value):
    high = value.astype(BF16)
    low = (value - high.astype(F32)).astype(BF16)
    return high, low


def split3(value):
    high = value.astype(BF16)
    rest = value - high.astype(F32)
    middle = rest.astype(BF16)
    low = (rest - middle.astype(F32)).astype(BF16)
    return high, middle, low


def dot_nn(left, right):
    left_h, left_l = split2(left)
    right_h, right_l = split2(right)
    return jnp.dot(
        jnp.concatenate([left_h, left_h, left_l], axis=1),
        jnp.concatenate([right_h, right_l, right_h], axis=0),
        preferred_element_type=F32,
    )


def dot_nt(left, right):
    left_h, left_l = split2(left)
    right_h, right_l = split2(right)
    return lax.dot_general(
        jnp.concatenate([left_h, left_h, left_l], axis=1),
        jnp.concatenate([right_h, right_l, right_h], axis=1),
        (((1,), (1,)), ((), ())),
        preferred_element_type=F32,
    )


def dot_exact(left_pieces, right):
    total = jnp.dot(left_pieces[0], right, preferred_element_type=F32)
    for piece in left_pieces[1:]:
        total = total + jnp.dot(piece, right, preferred_element_type=F32)
    return total


def sigmoid(value):
    return 1.0 / (1.0 + jnp.exp(-value))


def iota(axis, shape=(LANES, LANES)):
    return lax.broadcasted_iota(jnp.int32, shape, axis)


def shift_masks(seg_row):
    seg_cols = jnp.broadcast_to(seg_row.astype(F32), (LANES, LANES))
    seg_rows = seg_cols.T
    rows = iota(0)
    masks = []
    for offset in range(1, KCONV):
        prior = pltpu.roll(seg_rows, offset, 0)
        masks.append(jnp.where((rows >= offset) & (prior == seg_rows), 1.0, 0.0).astype(F32))
    return seg_rows, seg_cols, masks


def conv_silu(values, taps, masks):
    summed = taps[KCONV - 1 : KCONV] * values
    for offset in range(1, KCONV):
        shifted = pltpu.roll(values, offset, 0) * masks[offset - 1]
        summed = summed + taps[KCONV - 1 - offset : KCONV - offset] * shifted
    sig = sigmoid(summed)
    return summed * sig, sig * (1.0 + summed * (1.0 - sig))


def conv_back(cotangent, values, taps, masks):
    result = taps[KCONV - 1 : KCONV] * cotangent
    tap_grads = [None] * KCONV
    tap_grads[KCONV - 1] = jnp.sum(cotangent * values, axis=0, keepdims=True)
    for offset in range(1, KCONV):
        moved = pltpu.roll(cotangent * masks[offset - 1], LANES - offset, 0)
        result = result + taps[KCONV - 1 - offset : KCONV - offset] * moved
        tap_grads[KCONV - 1 - offset] = jnp.sum(moved * values, axis=0, keepdims=True)
    return result, tap_grads


def head_expander(heads):
    shape = (heads, heads * HDIM)
    return jnp.where(iota(1, shape) // HDIM == iota(0, shape), 1.0, 0.0).astype(BF16)


def two_halves(value):
    left = iota(1) < HDIM
    zero = jnp.zeros_like(value)
    return jnp.concatenate([jnp.where(left, value, zero), jnp.where(left, zero, value)], axis=0)


def staged(kernel, count, lazy):
    def run(meta_ref, *refs):
        inputs, rest = refs[:count], refs[count:]
        outputs, held, sems = rest[: -count - 1], rest[-count - 1 : -1], rest[-1]
        copies = [
            pltpu.make_async_copy(source, target, sems.at[i])
            for i, (source, target) in enumerate(zip(inputs, held))
        ]
        for copy in copies:
            copy.start()
        if lazy:
            kernel(meta_ref, copies, *held, *outputs)
        else:
            wait(copies)
            kernel(meta_ref, *held, *outputs)

    return run


def wait(copies):
    for copy in copies:
        copy.wait()


def place_pieces(meta_ref, refs, target):
    near, up, down, far0, far1 = refs
    pieces = [near.at[0], near.at[1], up.at[0], up.at[1], down.at[0], down.at[1], far0, far1]
    along, across = meta_ref[1], meta_ref[2]
    for piece, (far_x, far_y) in zip(pieces, PIECES):
        index = lax.rem(along + far_x, 4) * 2 + lax.bitwise_xor(across, far_y)
        target[:, :, pl.ds(pl.multiple_of(index * 16, 16), 16), :] = piece[...]


def forward_kernel(
    count_ref, z_ref, x_ref, b_ref, c_ref, dt_ref, seg_ref, cx_ref, cb_ref, cc_ref, al_ref, bias_ref, skip_ref, gain_ref,
    norm_ref, xc_ref, dsx_ref, ssm_ref, gate_ref, dgate_ref, bcc_ref, small_ref, cumt_ref, rms_ref,
):
    heads = dt_ref.shape[0]
    tiles = x_ref.shape[1] // LANES
    seg_rows, seg_cols, masks = shift_masks(seg_ref[...])
    rows, cols = iota(0), iota(1)
    causal = (rows >= cols) & (seg_rows == seg_cols)

    b_conv, b_slope = conv_silu(b_ref[...].astype(F32), cb_ref[...], masks)
    c_conv, c_slope = conv_silu(c_ref[...].astype(F32), cc_ref[...], masks)
    bcc_ref[0] = b_conv
    bcc_ref[1] = c_conv
    bcc_ref[2] = b_slope
    bcc_ref[3] = c_slope
    scores = dot_nt(c_conv, b_conv)
    bcc_ref[4] = scores.T

    raw = dt_ref[...].astype(F32).T + bias_ref[...]
    step = jnp.maximum(raw, 0.0) + jnp.log1p(jnp.exp(-jnp.abs(raw)))
    decay = -jnp.exp(al_ref[...]) * step
    lower = jnp.where(rows >= cols, 1.0, 0.0).astype(BF16)
    cumul = sum(jnp.dot(lower, piece, preferred_element_type=F32) for piece in split3(decay))
    cumul_t = cumul.T
    cumt_ref[...] = cumul_t
    small_ref[0] = step
    small_ref[1] = decay
    small_ref[2] = cumul
    small_ref[3] = sigmoid(raw)

    expander = head_expander(heads)
    step_wide = dot_exact(split3(step), expander)
    skip_wide = dot_exact(split3(jnp.broadcast_to(skip_ref[...], (8, heads))), expander)

    squares = jnp.zeros((LANES, LANES), F32)
    for tile in range(tiles):
        span = slice(tile * LANES, (tile + 1) * LANES)
        x_conv, x_slope = conv_silu(x_ref[:, span].astype(F32), cx_ref[:, span], masks)
        xc_ref[:, span] = x_conv
        dsx_ref[:, span] = x_slope
        pieces = []
        for head in (2 * tile, 2 * tile + 1):
            gap = cumul[:, head : head + 1] - cumul_t[head : head + 1, :]
            pieces.append(scores * jnp.exp(jnp.where(causal, gap, -1e30)))
        weights = jnp.concatenate(pieces, axis=1)
        ssm = dot_nn(weights, two_halves(step_wide[:, span] * x_conv))
        ssm = ssm + skip_wide[0:1, span] * x_conv
        ssm_ref[:, span] = ssm
        z_tile = z_ref[:, span].astype(F32)
        sig = sigmoid(z_tile)
        gate = z_tile * sig
        gate_ref[:, span] = gate
        dgate_ref[:, span] = sig * (1.0 + z_tile * (1.0 - sig))
        gated = ssm * gate
        squares = squares + gated * gated
    mean = jnp.sum(squares, axis=1, keepdims=True) / (tiles * LANES)
    inv = lax.rsqrt(jnp.broadcast_to(mean, (LANES, LANES)) + EPS)
    rms_ref[...] = inv
    alive = jnp.where(rows < count_ref[0], 1.0, 0.0).astype(F32)
    for tile in range(tiles):
        span = slice(tile * LANES, (tile + 1) * LANES)
        normed = ssm_ref[:, span] * gate_ref[:, span] * inv * gain_ref[:, span]
        norm_ref[:, span] = (normed * alive).astype(BF16)


def upstream_kernel(meta_ref, copies, near, up, down, far0, far1, *refs):
    *weights, own_ref, other_ref, rows_ref, sum_ref = refs
    wait(copies[:5])
    place_pieces(meta_ref, (near, up, down, far0, far1), rows_ref)
    for i, (block, shards) in enumerate(zip(weights, ring_order(meta_ref))):
        copies[5 + i].wait()
        left = [jnp.concatenate([rows_ref[who, k] for k in shards], axis=1) for who in range(2)]
        product = jnp.dot(jnp.concatenate(left, axis=0), block[...], preferred_element_type=F32)
        sum_ref[...] = product if i == 0 else sum_ref[...] + product
    length = own_ref.shape[0]
    own_ref[...] = sum_ref[:length, :]
    other_ref[...] = sum_ref[length:, :].astype(BF16)


def backward_kernel(meta_ref, own_ref, other_ref, *refs):
    *rest, up_ref = refs
    up_ref[...] = own_ref[...] + other_ref[...].astype(F32)
    pull_back(meta_ref, up_ref, *rest)


def ring_order(meta_ref):
    chip, core = meta_ref[3], meta_ref[4]
    other = 1 - core
    toward = 1 - 2 * core
    order = [(2 * chip + core, 2 * chip + other)]
    for k in (1, 2, 3):
        back = 2 * lax.rem(chip - toward * k + 8, 8)
        ahead = 2 * lax.rem(chip + toward * k + 8, 8)
        order += [(back + core, back + other), (ahead + other, ahead + core)]
    far = 2 * lax.rem(chip + 4, 8)
    return order + [(far + core,), (far + other,)]


def pull_back(
    count_ref, up_ref, x_ref, b_ref, c_ref, seg_ref, cx_ref, cb_ref, cc_ref, al_ref, skip_ref, gain_ref,
    xc_ref, dsx_ref, ssm_ref, gate_ref, dgate_ref, bcc_ref, small_ref, cumt_ref, rms_ref,
    gz_ref, gx_ref, gb_ref, gc_ref, gdt_ref, par_ref,
):
    heads = small_ref.shape[2]
    tiles = x_ref.shape[1] // LANES
    seg_rows, seg_cols, masks = shift_masks(seg_ref[...])
    rows, cols = iota(0), iota(1)
    causal_t = (cols >= rows) & (seg_rows == seg_cols)
    alive = jnp.where(rows < count_ref[0], 1.0, 0.0).astype(F32)
    inv = rms_ref[...]
    scores_t = bcc_ref[4]
    step, decay, cumul, slope = small_ref[0], small_ref[1], small_ref[2], small_ref[3]
    cumul_t = cumt_ref[...]
    expander = head_expander(heads)
    step_wide = dot_exact(split3(step), expander)
    skip_wide = dot_exact(split3(jnp.broadcast_to(skip_ref[...], (8, heads))), expander)

    dots = jnp.zeros((LANES, LANES), F32)
    for tile in range(tiles):
        span = slice(tile * LANES, (tile + 1) * LANES)
        upstream = up_ref[:, span] * alive
        gated = ssm_ref[:, span] * gate_ref[:, span]
        product = upstream * gated
        dots = dots + product * gain_ref[:, span]
        par_ref[32 + tile : 33 + tile, :] = jnp.sum(product * inv, axis=0, keepdims=True)
    mean = jnp.sum(dots, axis=1, keepdims=True) / (tiles * LANES)
    pull = jnp.broadcast_to(mean, (LANES, LANES)) * inv * inv * inv

    before = jnp.where(rows > cols, 1.0, 0.0).astype(BF16)
    before = jnp.concatenate([before, before], axis=1)
    after = jnp.where(cols >= rows, 1.0, 0.0).astype(F32)
    score_grad = jnp.zeros((LANES, LANES), F32)
    sums = jnp.zeros((LANES, LANES), F32)
    for tile in range(tiles):
        span = slice(tile * LANES, (tile + 1) * LANES)
        x_conv = xc_ref[:, span]
        ssm = ssm_ref[:, span]
        gate = gate_ref[:, span]
        d_gated = inv * (up_ref[:, span] * alive) * gain_ref[:, span] - ssm * gate * pull
        gz_ref[:, span] = (d_gated * ssm * dgate_ref[:, span]).astype(BF16)
        d_ssm = d_gated * gate
        x_step = step_wide[:, span] * x_conv
        d_weights = dot_nt(two_halves(x_step), d_ssm)
        pieces = []
        for which in range(2):
            head = 2 * tile + which
            gap = cumul_t[head : head + 1, :] - cumul[:, head : head + 1]
            fade = jnp.exp(jnp.where(causal_t, gap, -1e30))
            d_weight = d_weights[which * LANES : (which + 1) * LANES, :] * fade
            score_grad = score_grad + d_weight
            pieces.append((scores_t * fade, d_weight * scores_t))
        d_xstep = dot_nn(
            jnp.concatenate([pieces[0][0], pieces[1][0]], axis=1), two_halves(d_ssm)
        )
        gaps_h, gaps_l = split2(jnp.concatenate([pieces[0][1], pieces[1][1]], axis=1))
        gaps = jnp.dot(
            before, jnp.concatenate([gaps_h, gaps_l], axis=0), preferred_element_type=F32
        )
        terms = (
            gaps[:, :LANES] * after,
            gaps[:, LANES:] * after,
            d_xstep * x_conv,
            d_ssm * x_conv,
        )
        pickers = (
            jnp.where(cols == 2 * tile, 1.0, 0.0),
            jnp.where(cols == 2 * tile + 1, 1.0, 0.0),
            jnp.where(cols == heads + 2 * tile + rows // HDIM, 1.0, 0.0),
            jnp.where(cols == 2 * heads + 2 * tile + rows // HDIM, 1.0, 0.0),
        )
        left, right = [], []
        for term, picker in zip(terms, pickers):
            term_h, term_l = split2(term)
            left += [term_h, term_l]
            right += [picker.astype(BF16)] * 2
        sums = sums + jnp.dot(
            jnp.concatenate(left, axis=1),
            jnp.concatenate(right, axis=0),
            preferred_element_type=F32,
        )
        d_conv = skip_wide[0:1, span] * d_ssm + step_wide[:, span] * d_xstep
        x_grad, tap_grads = conv_back(
            d_conv * dsx_ref[:, span], x_ref[:, span].astype(F32), cx_ref[:, span], masks
        )
        gx_ref[:, span] = x_grad.astype(BF16)
        for tap in range(KCONV):
            par_ref[tap * tiles + tile : tap * tiles + tile + 1, :] = tap_grads[tap]

    d_decay = sums[:, 0:heads]
    d_step = sums[:, heads : 2 * heads] - jnp.exp(al_ref[...]) * d_decay
    d_raw = d_step * slope
    gdt_ref[...] = d_raw.T.astype(BF16)
    par_ref[48:49, 0:heads] = jnp.sum(d_decay * decay, axis=0, keepdims=True)
    par_ref[49:50, 0:heads] = jnp.sum(d_raw, axis=0, keepdims=True)
    par_ref[50:51, 0:heads] = jnp.sum(sums[:, 2 * heads : 3 * heads], axis=0, keepdims=True)

    b_conv, c_conv = bcc_ref[0], bcc_ref[1]
    b_grad, tap_grads = conv_back(
        dot_nn(score_grad, c_conv) * bcc_ref[2], b_ref[...].astype(F32), cb_ref[...], masks
    )
    gb_ref[...] = b_grad.astype(BF16)
    for tap in range(KCONV):
        par_ref[40 + tap : 41 + tap, :] = tap_grads[tap]
    c_grad, tap_grads = conv_back(
        dot_nn(score_grad.T, b_conv) * bcc_ref[3], c_ref[...].astype(F32), cc_ref[...], masks
    )
    gc_ref[...] = c_grad.astype(BF16)
    for tap in range(KCONV):
        par_ref[44 + tap : 45 + tap, :] = tap_grads[tap]


def unpack_kernel(par_ref, cx_ref, cb_ref, cc_ref, al_ref, bias_ref, skip_ref, gain_ref):
    heads = al_ref.shape[1]
    tiles = cx_ref.shape[1] // LANES
    total = par_ref[...]
    for tap in range(KCONV):
        for tile in range(tiles):
            cx_ref[tap : tap + 1, tile * LANES : (tile + 1) * LANES] = total[
                tap * tiles + tile : tap * tiles + tile + 1
            ]
    for tile in range(tiles):
        gain_ref[:, tile * LANES : (tile + 1) * LANES] = total[32 + tile : 33 + tile]
    cb_ref[...] = total[40:44]
    cc_ref[...] = total[44:48]
    al_ref[...] = total[48:49, 0:heads]
    bias_ref[...] = total[49:50, 0:heads]
    skip_ref[...] = total[50:51, 0:heads]


def weight_kernel(meta_ref, copies, near, up, down, far0, far1, own_ref, other_ref, keep_ref, give_ref, rows_ref):
    wait(copies)
    place_pieces(meta_ref, (near, up, down, far0, far1), rows_ref)
    chip, core = meta_ref[3], meta_ref[4]
    toward = 1 - 2 * core
    tokens = jnp.concatenate([own_ref[...], other_ref[...]], axis=0)
    for k in range(8):
        kept = 2 * lax.rem(chip + toward * k + 8, 8) + core
        given = 2 * lax.rem(chip - toward * k + 8, 8) + 1 - core
        left = [jnp.concatenate([rows_ref[who, kept], rows_ref[who, given]], axis=1) for who in range(2)]
        product = lax.dot_general(
            jnp.concatenate(left, axis=0), tokens, (((0,), (0,)), ((), ())), preferred_element_type=F32
        )
        depth = keep_ref.shape[1]
        keep_ref[k] = product[:depth]
        give_ref[k] = product[depth:].astype(BF16)


def call(kernel, operands, outs, flops, scratch=(), lazy=False):
    others = operands[1:]
    size = sum(a.size * a.dtype.itemsize for a in operands) + sum(
        a.size * a.dtype.itemsize for a in outs
    )
    return pl.pallas_call(
        staged(kernel, len(others), lazy),
        out_shape=outs,
        in_specs=[pl.BlockSpec(memory_space=pltpu.SMEM)] + [pl.BlockSpec(memory_space=pl.ANY)] * len(others),
        out_specs=[pl.BlockSpec(memory_space=pltpu.VMEM)] * len(outs),
        scratch_shapes=[
            *scratch,
            *[pltpu.VMEM(a.shape, a.dtype) for a in others],
            pltpu.SemaphoreType.DMA((len(others),)),
        ],
        compiler_params=pltpu.CompilerParams(vmem_limit_bytes=VMEM_LIMIT),
        cost_estimate=pl.CostEstimate(flops=flops, bytes_accessed=size, transcendentals=0),
    )(*operands)


def unpack(packed, outs):
    vmem = pl.BlockSpec(memory_space=pltpu.VMEM)
    return pl.pallas_call(
        unpack_kernel, out_shape=outs, in_specs=[vmem], out_specs=[vmem] * len(outs)
    )(packed)


def shape(dims, dtype=F32):
    return jax.ShapeDtypeStruct(dims, dtype)


def swap(value, axis, bit, size):
    return lax.ppermute(value, axis, [(i, i ^ bit) for i in range(size)])


def along_x(value, by):
    return lax.ppermute(value, "tensor", [(i, (i + 2 * by) % 8) for i in range(8)])


def gather_near(block):
    return jnp.stack([block, swap(block, "tensor", 1, 8)])


def gather_next(near):
    return along_x(near, 1), along_x(near, -1)


def gather_far(up, down):
    return along_x(up[0], 1), along_x(down[1], -1)


def after(value, *others):
    return lax.optimization_barrier((value, *others))[0]


def body(
    z_act, x_act, b_act, c_act, dt_act, segment, counts,
    conv_x, conv_b, conv_c, a_log, dt_bias, d_skip, norm_gain, w_out, d_out,
):
    length, width = z_act.shape
    heads = dt_act.shape[1]
    own, features = d_out.shape
    dp = lax.axis_size("dp")
    shard = lax.axis_index("dp")
    place = lax.axis_index("tensor")
    core = lax.bitwise_and(shard, 1)
    meta = jnp.stack(
        [counts[0], lax.shift_right_logical(place, 1), lax.bitwise_and(place, 1), lax.shift_right_logical(shard, 1), core]
    )
    chips = dp // 2
    ring = [(2 * z, 2 * ((z + 1) % chips)) for z in range(chips)]
    ring += [(2 * z + 1, 2 * ((z - 1) % chips) + 1) for z in range(chips)]
    seg_row = segment.reshape(1, length)
    a_log, dt_bias, d_skip = (v.reshape(1, heads) for v in (a_log, dt_bias, d_skip))
    gain = norm_gain.reshape(1, width)
    replica = lax.axis_index("rep")
    lower = replica == 0
    half = w_out.shape[0] // 2
    w_half = jnp.where(lower, w_out[:half], w_out[half:])
    pieces = d_out.reshape(own, dp, 2, half).transpose(2, 1, 0, 3)
    theirs = swap(jnp.where(lower, pieces[1], pieces[0]), "rep", 1, 2)
    mine = jnp.where(lower, pieces[0], pieces[1])
    def step(value):
        return lax.ppermute(value, "dp", ring)

    def back(value):
        return lax.ppermute(value, "dp", [(j, i) for i, j in ring])

    def across(*values):
        return [swap(value, "dp", 1, dp) for value in values]

    wide = shape((length, width))
    normed, *saved = call(
        forward_kernel,
        (meta, z_act, x_act, b_act, c_act, dt_act.T, seg_row, conv_x, conv_b, conv_c, a_log, dt_bias, d_skip, gain),
        [
            shape((length, width), BF16), wide, wide, wide, wide, wide,
            shape((5, LANES, LANES)), shape((4, length, heads)), shape((heads, length)), shape((LANES, LANES)),
        ],
        5_000_000_000,
    )

    def pair_up(block):
        return jnp.concatenate([block, *across(block)], axis=0)

    def passed(rounds, single):
        held = [rounds[0]]
        for pair in rounds[1:]:
            held += [pair, *across(pair)]
        return held + [single, *across(single)]

    weights = [pair_up(w_half)]
    for _ in range(3):
        weights.append(step(weights[-1]))
    near = gather_near(after(jnp.stack([mine, theirs]), weights[0]))
    up, down = gather_next(after(near, weights[1]))
    rows = (near, up, down, *gather_far(after(up, weights[2]), down))

    keep, give = call(
        weight_kernel,
        (meta, *rows, after(normed, weights[3]), swap(normed, "rep", 1, 2)),
        [shape((chips, half, width)), shape((chips, half, width), BF16)],
        5_000_000_000,
        lazy=True,
        scratch=[pltpu.VMEM((2, dp, length, half), BF16)],
    )
    weights = passed(weights, step(weights[-1][:half]))
    (given,) = across(give)

    def term(k):
        return keep[k] + given[k].astype(F32)

    upstream, other = call(
        upstream_kernel,
        (meta, *rows, *weights),
        [shape((length, width)), shape((length, width), BF16)],
        4_000_000_000,
        lazy=True,
        scratch=[pltpu.VMEM((2, dp, length, half), BF16), pltpu.VMEM((2 * length, width), F32)],
    )
    one, two = term(4), term(5)
    one = step(one.astype(BF16)).astype(F32) + term(3)
    two = back(two.astype(BF16)).astype(F32) + term(6)
    one, two = after(one, other), after(two, other)
    other = swap(other, "rep", 1, 2)

    *act_grads, packed = call(
        backward_kernel,
        (
            meta, upstream, other,
            x_act, b_act, c_act, seg_row, conv_x, conv_b, conv_c, a_log, d_skip, gain, *saved,
        ),
        [
            shape((length, width), BF16), shape((length, width), BF16), shape((length, LANES), BF16),
            shape((length, LANES), BF16), shape((heads, length), BF16), shape((56, LANES)),
        ],
        10_000_000_000,
        scratch=[pltpu.VMEM((length, width), F32)],
    )
    act_grads[4] = act_grads[4].T
    one = step(one.astype(BF16)).astype(F32) + term(2)
    two = back(two.astype(BF16)).astype(F32) + term(7)
    one, two = after(one, packed), after(two, packed)
    one = step(one.astype(BF16)).astype(F32) + term(1)
    two = back(two.astype(BF16)).astype(F32)
    packed = packed + swap(packed, "dp", 1, dp)
    packed = packed + swap(packed, "dp", 2, dp)
    total = (term(0) + two + step(after(one, packed).astype(BF16)).astype(F32)).astype(BF16)
    packed = packed + swap(packed, "rep", 1, 2)
    packed = packed + swap(packed, "dp", 4, dp)
    partner = swap(after(total, packed), "rep", 1, 2)
    weight_grad = jnp.concatenate(
        [jnp.where(lower, total, partner), jnp.where(lower, partner, total)], axis=0
    ).astype(F32)
    packed = packed + swap(packed, "dp", 8, dp)
    sums = unpack(
        packed,
        [
            shape(conv_x.shape), shape(conv_b.shape), shape(conv_c.shape),
            shape((1, heads)), shape((1, heads)), shape((1, heads)), shape((1, width)),
        ],
    )

    return (
        *act_grads,
        sums[0], sums[1], sums[2],
        sums[3].reshape(heads), sums[4].reshape(heads), sums[5].reshape(heads), sums[6].reshape(width),
        weight_grad,
    )


def solution(mesh):
    tokens = P(("rep", "dp"), "tensor")
    shards = P(("rep", "dp"))
    taps = P(None, "tensor")
    per_head = P("tensor")
    weight = P("dp", "tensor")
    in_specs = (
        *([tokens] * 5), shards, shards, *([taps] * 3), *([per_head] * 4),
        weight, P(("rep", "dp", "tensor"), None),
    )
    out_specs = (*([tokens] * 5), *([taps] * 3), *([per_head] * 4), weight)
    return jax.shard_map(body, mesh=mesh, in_specs=in_specs, out_specs=out_specs, check_vma=False)
```

```python
import jax
import jax.numpy as jnp
from jax import lax
from jax.experimental import pallas as pl
from jax.experimental.pallas import tpu as pltpu
from jax.sharding import PartitionSpec as P

HDIM = 64
LANES = 128
KCONV = 4
EPS = 1e-05
F32 = jnp.float32
BF16 = jnp.bfloat16
VMEM_LIMIT = 56 * 1024 * 1024
SHARDS = 16
PIECES = ((0, 0), (0, 1), (3, 0), (3, 1), (1, 0), (1, 1), (2, 0), (2, 1))


def split2(value):
    high = value.astype(BF16)
    low = (value - high.astype(F32)).astype(BF16)
    return high, low


def split3(value):
    high = value.astype(BF16)
    rest = value - high.astype(F32)
    middle = rest.astype(BF16)
    low = (rest - middle.astype(F32)).astype(BF16)
    return high, middle, low


def dot_nn(left, right):
    left_h, left_l = split2(left)
    right_h, right_l = split2(right)
    return jnp.dot(
        jnp.concatenate([left_h, left_h, left_l], axis=1),
        jnp.concatenate([right_h, right_l, right_h], axis=0),
        preferred_element_type=F32,
    )


def dot_nt(left, right):
    left_h, left_l = split2(left)
    right_h, right_l = split2(right)
    return lax.dot_general(
        jnp.concatenate([left_h, left_h, left_l], axis=1),
        jnp.concatenate([right_h, right_l, right_h], axis=1),
        (((1,), (1,)), ((), ())),
        preferred_element_type=F32,
    )


def dot_exact(left_pieces, right):
    total = jnp.dot(left_pieces[0], right, preferred_element_type=F32)
    for piece in left_pieces[1:]:
        total = total + jnp.dot(piece, right, preferred_element_type=F32)
    return total


def sigmoid(value):
    return 1.0 / (1.0 + jnp.exp(-value))


def iota(axis, shape=(LANES, LANES)):
    return lax.broadcasted_iota(jnp.int32, shape, axis)


def shift_masks(seg_row):
    seg_cols = jnp.broadcast_to(seg_row.astype(F32), (LANES, LANES))
    seg_rows = seg_cols.T
    rows = iota(0)
    masks = []
    for offset in range(1, KCONV):
        prior = pltpu.roll(seg_rows, offset, 0)
        masks.append(jnp.where((rows >= offset) & (prior == seg_rows), 1.0, 0.0).astype(F32))
    return seg_rows, seg_cols, masks


def conv_silu(values, taps, masks):
    summed = taps[KCONV - 1 : KCONV] * values
    for offset in range(1, KCONV):
        shifted = pltpu.roll(values, offset, 0) * masks[offset - 1]
        summed = summed + taps[KCONV - 1 - offset : KCONV - offset] * shifted
    sig = sigmoid(summed)
    return summed * sig, sig * (1.0 + summed * (1.0 - sig))


def conv_back(cotangent, values, taps, masks):
    result = taps[KCONV - 1 : KCONV] * cotangent
    tap_grads = [None] * KCONV
    tap_grads[KCONV - 1] = jnp.sum(cotangent * values, axis=0, keepdims=True)
    for offset in range(1, KCONV):
        moved = pltpu.roll(cotangent * masks[offset - 1], LANES - offset, 0)
        result = result + taps[KCONV - 1 - offset : KCONV - offset] * moved
        tap_grads[KCONV - 1 - offset] = jnp.sum(moved * values, axis=0, keepdims=True)
    return result, tap_grads


def head_expander(heads):
    shape = (heads, heads * HDIM)
    return jnp.where(iota(1, shape) // HDIM == iota(0, shape), 1.0, 0.0).astype(BF16)


def two_halves(value):
    left = iota(1) < HDIM
    zero = jnp.zeros_like(value)
    return jnp.concatenate([jnp.where(left, value, zero), jnp.where(left, zero, value)], axis=0)


def staged(kernel, count, lazy):
    def run(meta_ref, *refs):
        inputs, rest = refs[:count], refs[count:]
        outputs, held, sems = rest[: -count - 1], rest[-count - 1 : -1], rest[-1]
        copies = [
            pltpu.make_async_copy(source, target, sems.at[i])
            for i, (source, target) in enumerate(zip(inputs, held))
        ]
        for copy in copies:
            copy.start()
        if lazy:
            kernel(meta_ref, copies, *held, *outputs)
        else:
            wait(copies)
            kernel(meta_ref, *held, *outputs)

    return run


def wait(copies):
    for copy in copies:
        copy.wait()


def place_pieces(meta_ref, refs, target):
    near, up, down, far0, far1 = refs
    pieces = [near.at[0], near.at[1], up.at[0], up.at[1], down.at[0], down.at[1], far0, far1]
    along, across = meta_ref[1], meta_ref[2]
    for piece, (far_x, far_y) in zip(pieces, PIECES):
        index = lax.rem(along + far_x, 4) * 2 + lax.bitwise_xor(across, far_y)
        target[:, :, pl.ds(pl.multiple_of(index * 16, 16), 16), :] = piece[...]


def forward_kernel(
    count_ref, z_ref, x_ref, b_ref, c_ref, dt_ref, seg_ref, cx_ref, cb_ref, cc_ref, al_ref, bias_ref, skip_ref, gain_ref,
    norm_ref, xc_ref, dsx_ref, ssm_ref, gate_ref, dgate_ref, bcc_ref, small_ref, cumt_ref, rms_ref,
):
    heads = dt_ref.shape[0]
    tiles = x_ref.shape[1] // LANES
    seg_rows, seg_cols, masks = shift_masks(seg_ref[...])
    rows, cols = iota(0), iota(1)
    causal = (rows >= cols) & (seg_rows == seg_cols)

    b_conv, b_slope = conv_silu(b_ref[...].astype(F32), cb_ref[...], masks)
    c_conv, c_slope = conv_silu(c_ref[...].astype(F32), cc_ref[...], masks)
    bcc_ref[0] = b_conv
    bcc_ref[1] = c_conv
    bcc_ref[2] = b_slope
    bcc_ref[3] = c_slope
    scores = dot_nt(c_conv, b_conv)
    bcc_ref[4] = scores.T

    raw = dt_ref[...].astype(F32).T + bias_ref[...]
    step = jnp.maximum(raw, 0.0) + jnp.log1p(jnp.exp(-jnp.abs(raw)))
    decay = -jnp.exp(al_ref[...]) * step
    lower = jnp.where(rows >= cols, 1.0, 0.0).astype(BF16)
    cumul = sum(jnp.dot(lower, piece, preferred_element_type=F32) for piece in split3(decay))
    cumul_t = cumul.T
    cumt_ref[...] = cumul_t
    small_ref[0] = step
    small_ref[1] = decay
    small_ref[2] = cumul
    small_ref[3] = sigmoid(raw)

    expander = head_expander(heads)
    step_wide = dot_exact(split3(step), expander)
    skip_wide = dot_exact(split3(jnp.broadcast_to(skip_ref[...], (8, heads))), expander)

    squares = jnp.zeros((LANES, LANES), F32)
    for tile in range(tiles):
        span = slice(tile * LANES, (tile + 1) * LANES)
        x_conv, x_slope = conv_silu(x_ref[:, span].astype(F32), cx_ref[:, span], masks)
        xc_ref[:, span] = x_conv
        dsx_ref[:, span] = x_slope
        pieces = []
        for head in (2 * tile, 2 * tile + 1):
            gap = cumul[:, head : head + 1] - cumul_t[head : head + 1, :]
            pieces.append(scores * jnp.exp(jnp.where(causal, gap, -1e30)))
        weights = jnp.concatenate(pieces, axis=1)
        ssm = dot_nn(weights, two_halves(step_wide[:, span] * x_conv))
        ssm = ssm + skip_wide[0:1, span] * x_conv
        ssm_ref[:, span] = ssm
        z_tile = z_ref[:, span].astype(F32)
        sig = sigmoid(z_tile)
        gate = z_tile * sig
        gate_ref[:, span] = gate
        dgate_ref[:, span] = sig * (1.0 + z_tile * (1.0 - sig))
        gated = ssm * gate
        squares = squares + gated * gated
    mean = jnp.sum(squares, axis=1, keepdims=True) / (tiles * LANES)
    inv = lax.rsqrt(jnp.broadcast_to(mean, (LANES, LANES)) + EPS)
    rms_ref[...] = inv
    alive = jnp.where(rows < count_ref[0], 1.0, 0.0).astype(F32)
    for tile in range(tiles):
        span = slice(tile * LANES, (tile + 1) * LANES)
        normed = ssm_ref[:, span] * gate_ref[:, span] * inv * gain_ref[:, span]
        norm_ref[:, span] = (normed * alive).astype(BF16)


def upstream_kernel(meta_ref, copies, near, up, down, far0, far1, *refs):
    *weights, own_ref, other_ref, rows_ref, sum_ref = refs
    wait(copies[:5])
    place_pieces(meta_ref, (near, up, down, far0, far1), rows_ref)
    for i, (block, shards) in enumerate(zip(weights, ring_order(meta_ref))):
        copies[5 + i].wait()
        left = [jnp.concatenate([rows_ref[who, k] for k in shards], axis=1) for who in range(2)]
        product = jnp.dot(jnp.concatenate(left, axis=0), block[...], preferred_element_type=F32)
        sum_ref[...] = product if i == 0 else sum_ref[...] + product
    length = own_ref.shape[0]
    own_ref[...] = sum_ref[:length, :]
    other_ref[...] = sum_ref[length:, :].astype(BF16)


def backward_kernel(meta_ref, own_ref, other_ref, *refs):
    *rest, up_ref = refs
    up_ref[...] = own_ref[...] + other_ref[...].astype(F32)
    pull_back(meta_ref, up_ref, *rest)


def ring_order(meta_ref):
    chip, core = meta_ref[3], meta_ref[4]
    other = 1 - core
    toward = 1 - 2 * core
    order = [(2 * chip + core, 2 * chip + other)]
    for k in (1, 2, 3):
        back = 2 * lax.rem(chip - toward * k + 8, 8)
        ahead = 2 * lax.rem(chip + toward * k + 8, 8)
        order += [(back + core, back + other), (ahead + other, ahead + core)]
    far = 2 * lax.rem(chip + 4, 8)
    return order + [(far + core,), (far + other,)]


def pull_back(
    count_ref, up_ref, x_ref, b_ref, c_ref, seg_ref, cx_ref, cb_ref, cc_ref, al_ref, skip_ref, gain_ref,
    xc_ref, dsx_ref, ssm_ref, gate_ref, dgate_ref, bcc_ref, small_ref, cumt_ref, rms_ref,
    gz_ref, gx_ref, gb_ref, gc_ref, gdt_ref, par_ref,
):
    heads = small_ref.shape[2]
    tiles = x_ref.shape[1] // LANES
    seg_rows, seg_cols, masks = shift_masks(seg_ref[...])
    rows, cols = iota(0), iota(1)
    causal_t = (cols >= rows) & (seg_rows == seg_cols)
    alive = jnp.where(rows < count_ref[0], 1.0, 0.0).astype(F32)
    inv = rms_ref[...]
    scores_t = bcc_ref[4]
    step, decay, cumul, slope = small_ref[0], small_ref[1], small_ref[2], small_ref[3]
    cumul_t = cumt_ref[...]
    expander = head_expander(heads)
    step_wide = dot_exact(split3(step), expander)
    skip_wide = dot_exact(split3(jnp.broadcast_to(skip_ref[...], (8, heads))), expander)

    dots = jnp.zeros((LANES, LANES), F32)
    for tile in range(tiles):
        span = slice(tile * LANES, (tile + 1) * LANES)
        upstream = up_ref[:, span] * alive
        gated = ssm_ref[:, span] * gate_ref[:, span]
        product = upstream * gated
        dots = dots + product * gain_ref[:, span]
        par_ref[32 + tile : 33 + tile, :] = jnp.sum(product * inv, axis=0, keepdims=True)
    mean = jnp.sum(dots, axis=1, keepdims=True) / (tiles * LANES)
    pull = jnp.broadcast_to(mean, (LANES, LANES)) * inv * inv * inv

    before = jnp.where(rows > cols, 1.0, 0.0).astype(BF16)
    before = jnp.concatenate([before, before], axis=1)
    after = jnp.where(cols >= rows, 1.0, 0.0).astype(F32)
    score_grad = jnp.zeros((LANES, LANES), F32)
    sums = jnp.zeros((LANES, LANES), F32)
    for tile in range(tiles):
        span = slice(tile * LANES, (tile + 1) * LANES)
        x_conv = xc_ref[:, span]
        ssm = ssm_ref[:, span]
        gate = gate_ref[:, span]
        d_gated = inv * (up_ref[:, span] * alive) * gain_ref[:, span] - ssm * gate * pull
        gz_ref[:, span] = (d_gated * ssm * dgate_ref[:, span]).astype(BF16)
        d_ssm = d_gated * gate
        x_step = step_wide[:, span] * x_conv
        d_weights = dot_nt(two_halves(x_step), d_ssm)
        pieces = []
        for which in range(2):
            head = 2 * tile + which
            gap = cumul_t[head : head + 1, :] - cumul[:, head : head + 1]
            fade = jnp.exp(jnp.where(causal_t, gap, -1e30))
            d_weight = d_weights[which * LANES : (which + 1) * LANES, :] * fade
            score_grad = score_grad + d_weight
            pieces.append((scores_t * fade, d_weight * scores_t))
        d_xstep = dot_nn(
            jnp.concatenate([pieces[0][0], pieces[1][0]], axis=1), two_halves(d_ssm)
        )
        gaps_h, gaps_l = split2(jnp.concatenate([pieces[0][1], pieces[1][1]], axis=1))
        gaps = jnp.dot(
            before, jnp.concatenate([gaps_h, gaps_l], axis=0), preferred_element_type=F32
        )
        terms = (
            gaps[:, :LANES] * after,
            gaps[:, LANES:] * after,
            d_xstep * x_conv,
            d_ssm * x_conv,
        )
        pickers = (
            jnp.where(cols == 2 * tile, 1.0, 0.0),
            jnp.where(cols == 2 * tile + 1, 1.0, 0.0),
            jnp.where(cols == heads + 2 * tile + rows // HDIM, 1.0, 0.0),
            jnp.where(cols == 2 * heads + 2 * tile + rows // HDIM, 1.0, 0.0),
        )
        left, right = [], []
        for term, picker in zip(terms, pickers):
            term_h, term_l = split2(term)
            left += [term_h, term_l]
            right += [picker.astype(BF16)] * 2
        sums = sums + jnp.dot(
            jnp.concatenate(left, axis=1),
            jnp.concatenate(right, axis=0),
            preferred_element_type=F32,
        )
        d_conv = skip_wide[0:1, span] * d_ssm + step_wide[:, span] * d_xstep
        x_grad, tap_grads = conv_back(
            d_conv * dsx_ref[:, span], x_ref[:, span].astype(F32), cx_ref[:, span], masks
        )
        gx_ref[:, span] = x_grad.astype(BF16)
        for tap in range(KCONV):
            par_ref[tap * tiles + tile : tap * tiles + tile + 1, :] = tap_grads[tap]

    d_decay = sums[:, 0:heads]
    d_step = sums[:, heads : 2 * heads] - jnp.exp(al_ref[...]) * d_decay
    d_raw = d_step * slope
    gdt_ref[...] = d_raw.T.astype(BF16)
    par_ref[48:49, 0:heads] = jnp.sum(d_decay * decay, axis=0, keepdims=True)
    par_ref[49:50, 0:heads] = jnp.sum(d_raw, axis=0, keepdims=True)
    par_ref[50:51, 0:heads] = jnp.sum(sums[:, 2 * heads : 3 * heads], axis=0, keepdims=True)

    b_conv, c_conv = bcc_ref[0], bcc_ref[1]
    b_grad, tap_grads = conv_back(
        dot_nn(score_grad, c_conv) * bcc_ref[2], b_ref[...].astype(F32), cb_ref[...], masks
    )
    gb_ref[...] = b_grad.astype(BF16)
    for tap in range(KCONV):
        par_ref[40 + tap : 41 + tap, :] = tap_grads[tap]
    c_grad, tap_grads = conv_back(
        dot_nn(score_grad.T, b_conv) * bcc_ref[3], c_ref[...].astype(F32), cc_ref[...], masks
    )
    gc_ref[...] = c_grad.astype(BF16)
    for tap in range(KCONV):
        par_ref[44 + tap : 45 + tap, :] = tap_grads[tap]


def unpack_kernel(par_ref, far_ref, cx_ref, cb_ref, cc_ref, al_ref, bias_ref, skip_ref, gain_ref):
    heads = al_ref.shape[1]
    tiles = cx_ref.shape[1] // LANES
    total = par_ref[...] + far_ref[...]
    for tap in range(KCONV):
        for tile in range(tiles):
            cx_ref[tap : tap + 1, tile * LANES : (tile + 1) * LANES] = total[
                tap * tiles + tile : tap * tiles + tile + 1
            ]
    for tile in range(tiles):
        gain_ref[:, tile * LANES : (tile + 1) * LANES] = total[32 + tile : 33 + tile]
    cb_ref[...] = total[40:44]
    cc_ref[...] = total[44:48]
    al_ref[...] = total[48:49, 0:heads]
    bias_ref[...] = total[49:50, 0:heads]
    skip_ref[...] = total[50:51, 0:heads]


def weight_kernel(meta_ref, copies, near, up, down, far0, far1, own_ref, other_ref, keep_ref, give_ref, rows_ref):
    wait(copies)
    place_pieces(meta_ref, (near, up, down, far0, far1), rows_ref)
    chip, core = meta_ref[3], meta_ref[4]
    toward = 1 - 2 * core
    tokens = jnp.concatenate([own_ref[...], other_ref[...]], axis=0)
    for k in range(8):
        kept = 2 * lax.rem(chip + toward * k + 8, 8) + core
        given = 2 * lax.rem(chip - toward * k + 8, 8) + 1 - core
        left = [jnp.concatenate([rows_ref[who, kept], rows_ref[who, given]], axis=1) for who in range(2)]
        product = lax.dot_general(
            jnp.concatenate(left, axis=0), tokens, (((0,), (0,)), ((), ())), preferred_element_type=F32
        )
        depth = keep_ref.shape[1]
        keep_ref[k] = product[:depth]
        give_ref[k] = product[depth:].astype(BF16)


def call(kernel, operands, outs, flops, scratch=(), lazy=False):
    others = operands[1:]
    size = sum(a.size * a.dtype.itemsize for a in operands) + sum(
        a.size * a.dtype.itemsize for a in outs
    )
    return pl.pallas_call(
        staged(kernel, len(others), lazy),
        out_shape=outs,
        in_specs=[pl.BlockSpec(memory_space=pltpu.SMEM)] + [pl.BlockSpec(memory_space=pl.ANY)] * len(others),
        out_specs=[pl.BlockSpec(memory_space=pltpu.VMEM)] * len(outs),
        scratch_shapes=[
            *scratch,
            *[pltpu.VMEM(a.shape, a.dtype) for a in others],
            pltpu.SemaphoreType.DMA((len(others),)),
        ],
        compiler_params=pltpu.CompilerParams(vmem_limit_bytes=VMEM_LIMIT),
        cost_estimate=pl.CostEstimate(flops=flops, bytes_accessed=size, transcendentals=0),
    )(*operands)


def unpack(packed, far, outs):
    vmem = pl.BlockSpec(memory_space=pltpu.VMEM)
    return pl.pallas_call(
        unpack_kernel, out_shape=outs, in_specs=[vmem] * 2, out_specs=[vmem] * len(outs)
    )(packed, far)


def shape(dims, dtype=F32):
    return jax.ShapeDtypeStruct(dims, dtype)


def swap(value, axis, bit, size):
    return lax.ppermute(value, axis, [(i, i ^ bit) for i in range(size)])


def along_x(value, by):
    return lax.ppermute(value, "tensor", [(i, (i + 2 * by) % 8) for i in range(8)])


def gather_near(block):
    return jnp.stack([block, swap(block, "tensor", 1, 8)])


def gather_next(near):
    return along_x(near, 1), along_x(near, -1)


def gather_far(up, down):
    return along_x(up[0], 1), along_x(down[1], -1)


def after(value, *others):
    return lax.optimization_barrier((value, *others))[0]


def body(
    z_act, x_act, b_act, c_act, dt_act, segment, counts,
    conv_x, conv_b, conv_c, a_log, dt_bias, d_skip, norm_gain, w_out, d_out,
):
    length, width = z_act.shape
    heads = dt_act.shape[1]
    own, features = d_out.shape
    dp = lax.axis_size("dp")
    shard = lax.axis_index("dp")
    place = lax.axis_index("tensor")
    core = lax.bitwise_and(shard, 1)
    meta = jnp.stack(
        [counts[0], lax.shift_right_logical(place, 1), lax.bitwise_and(place, 1), lax.shift_right_logical(shard, 1), core]
    )
    chips = dp // 2
    ring = [(2 * z, 2 * ((z + 1) % chips)) for z in range(chips)]
    ring += [(2 * z + 1, 2 * ((z - 1) % chips) + 1) for z in range(chips)]
    seg_row = segment.reshape(1, length)
    a_log, dt_bias, d_skip = (v.reshape(1, heads) for v in (a_log, dt_bias, d_skip))
    gain = norm_gain.reshape(1, width)
    replica = lax.axis_index("rep")
    lower = replica == 0
    half = w_out.shape[0] // 2
    w_half = jnp.where(lower, w_out[:half], w_out[half:])
    pieces = d_out.reshape(own, dp, 2, half).transpose(2, 1, 0, 3)
    theirs = swap(jnp.where(lower, pieces[1], pieces[0]), "rep", 1, 2)
    mine = jnp.where(lower, pieces[0], pieces[1])
    def step(value):
        return lax.ppermute(value, "dp", ring)

    def back(value):
        return lax.ppermute(value, "dp", [(j, i) for i, j in ring])

    def across(*values):
        return [swap(value, "dp", 1, dp) for value in values]

    wide = shape((length, width))
    normed, *saved = call(
        forward_kernel,
        (meta, z_act, x_act, b_act, c_act, dt_act.T, seg_row, conv_x, conv_b, conv_c, a_log, dt_bias, d_skip, gain),
        [
            shape((length, width), BF16), wide, wide, wide, wide, wide,
            shape((5, LANES, LANES)), shape((4, length, heads)), shape((heads, length)), shape((LANES, LANES)),
        ],
        5_000_000_000,
    )

    def pair_up(block):
        return jnp.concatenate([block, *across(block)], axis=0)

    def passed(rounds, single):
        held = [rounds[0]]
        for pair in rounds[1:]:
            held += [pair, *across(pair)]
        return held + [single, *across(single)]

    weights = [pair_up(w_half)]
    for _ in range(3):
        weights.append(step(weights[-1]))
    near = gather_near(after(jnp.stack([mine, theirs]), weights[0]))
    up, down = gather_next(after(near, weights[1]))
    rows = (near, up, down, *gather_far(after(up, weights[2]), down))

    keep, give = call(
        weight_kernel,
        (meta, *rows, after(normed, weights[3]), swap(normed, "rep", 1, 2)),
        [shape((chips, half, width)), shape((chips, half, width), BF16)],
        5_000_000_000,
        lazy=True,
        scratch=[pltpu.VMEM((2, dp, length, half), BF16)],
    )
    weights = passed(weights, step(weights[-1][:half]))
    (given,) = across(give)

    def term(k):
        return keep[k] + given[k].astype(F32)

    upstream, other = call(
        upstream_kernel,
        (meta, *rows, *weights),
        [shape((length, width)), shape((length, width), BF16)],
        4_000_000_000,
        lazy=True,
        scratch=[pltpu.VMEM((2, dp, length, half), BF16), pltpu.VMEM((2 * length, width), F32)],
    )
    one, two = term(4), term(5)
    one = step(one.astype(BF16)).astype(F32) + term(3)
    two = back(two.astype(BF16)).astype(F32) + term(6)
    one, two = after(one, other), after(two, other)
    other = swap(other, "rep", 1, 2)

    *act_grads, packed = call(
        backward_kernel,
        (
            meta, upstream, other,
            x_act, b_act, c_act, seg_row, conv_x, conv_b, conv_c, a_log, d_skip, gain, *saved,
        ),
        [
            shape((length, width), BF16), shape((length, width), BF16), shape((length, LANES), BF16),
            shape((length, LANES), BF16), shape((heads, length), BF16), shape((56, LANES)),
        ],
        10_000_000_000,
        scratch=[pltpu.VMEM((length, width), F32)],
    )
    act_grads[4] = act_grads[4].T
    one = step(one.astype(BF16)).astype(F32) + term(2)
    two = back(two.astype(BF16)).astype(F32) + term(7)
    one, two = after(one, packed), after(two, packed)
    one = step(one.astype(BF16)).astype(F32) + term(1)
    two = back(two.astype(BF16)).astype(F32)
    packed = packed + swap(packed, "dp", 1, dp)
    packed = packed + swap(packed, "dp", 2, dp)
    total = (term(0) + two + step(after(one, packed).astype(BF16)).astype(F32)).astype(BF16)
    packed = packed + swap(packed, "rep", 1, 2)
    packed = packed + swap(packed, "dp", 4, dp)
    partner = swap(after(total, packed), "rep", 1, 2)
    weight_grad = jnp.concatenate(
        [jnp.where(lower, total, partner), jnp.where(lower, partner, total)], axis=0
    ).astype(F32)
    far = swap(packed, "dp", 8, dp)
    sums = unpack(
        after(packed, weight_grad),
        far,
        [
            shape(conv_x.shape), shape(conv_b.shape), shape(conv_c.shape),
            shape((1, heads)), shape((1, heads)), shape((1, heads)), shape((1, width)),
        ],
    )

    return (
        *act_grads,
        sums[0], sums[1], sums[2],
        sums[3].reshape(heads), sums[4].reshape(heads), sums[5].reshape(heads), sums[6].reshape(width),
        weight_grad,
    )


def solution(mesh):
    tokens = P(("rep", "dp"), "tensor")
    shards = P(("rep", "dp"))
    taps = P(None, "tensor")
    per_head = P("tensor")
    weight = P("dp", "tensor")
    in_specs = (
        *([tokens] * 5), shards, shards, *([taps] * 3), *([per_head] * 4),
        weight, P(("rep", "dp", "tensor"), None),
    )
    out_specs = (*([tokens] * 5), *([taps] * 3), *([per_head] * 4), weight)
    return jax.shard_map(body, mesh=mesh, in_specs=in_specs, out_specs=out_specs, check_vma=False)
```
